256 devices in a mesh: frame: 32 (over z, x_hi, core), head: 8 (over y, x_lo).
Axes of the slice: x: 4 (x_hi: 2, x_lo: 2; x = x_hi * 2 + x_lo), y: 4, z: 8, core: 2. Of those that a mesh axis runs over, the one named last changes fastest.
Arguments:
- queue: bfloat16 [4096, 5120], P('frame', 'head'), may hold values from -6 to 6
- noise_block: bfloat16 [64, 5120], P(None, 'head'), may hold values from -6 to 6
- w_query: bfloat16 [5120, 3072], P('frame', 'head'), may hold values from -0.078125 to 0.078125
- w_key: bfloat16 [5120, 3072], P('frame', 'head'), may hold values from -0.078125 to 0.078125
- w_value: bfloat16 [5120, 3072], P('frame', 'head'), may hold values from -0.078125 to 0.078125
- w_output: bfloat16 [3072, 5120], P('head', 'frame'), may hold values from -1.5 to 1.5
- mod_table: float32 [64, 3, 5120], replicated, may hold values from -4 to 4
- sigma_table: float32 [65], replicated, may hold values from 0 to 1
- timestep_index: int32 [64], P('frame'), may hold values from 0 to 63
- block_position: int32 [64], P('frame'), may hold values from 0 to 4095
Outputs:
- velocity: bfloat16 [4096, 5120], P('frame', 'head')
- queue_out: bfloat16 [4096, 5120], P('frame', 'head')
The draws below stay inside these ranges and needn't reach their ends.
All inputs are finite; a program needn't handle non-finite values.
Results may differ from the reference program's by a relative error of at most 0.025.
Values may be sent and summed in bfloat16 or wider, within the bound.
No kernel may reach another device: no remote copies, remote signals or barrier semaphores. Data moves between devices by JAX's collectives and lax.ppermute only.
A program may use at most 128 MiB of HBM per device.

```python
import math
import jax
import jax.numpy as jnp
from jax import lax

D = 5120
HEAD_SIZE = 128
HEAD_DEV = 3
REACH = 2
TOK_CH = 64
LEVELS = 64
HEADS = 24
BLOCKS = 64
TOKENS = 4096
N_HEAD = 8


def touch_ends(values, stream_key, smallest, top_value):
    longest = values.shape.index(max(values.shape))
    spots = []
    for shift in (0, 1):
        where = [jax.random.randint(jax.random.fold_in(stream_key, axis), (), 0, length) for axis, length in enumerate(values.shape)]
        where[longest] = (where[longest] + shift) % values.shape[longest]
        spots.append(tuple(where))
    return values.at[spots[0]].set(smallest).at[spots[1]].set(top_value)


def level_of(rng, dims, split, low, largest):
    def one(axis_at, shards_of):
        steps = jax.random.uniform(jax.random.fold_in(jax.random.fold_in(rng, 6), axis_at), (shards_of,), jnp.float32, low / len(split), largest / len(split))
        return jnp.repeat(jnp.exp(steps), dims[axis_at] // shards_of).reshape((-1,) + (1,) * (len(dims) - axis_at - 1))

    level = one(*split[0])
    for cut in split[1:]:
        level = level * one(*cut)
    return level


def scatter_about(rng, extent, spread, most, pieces=(), held_as=jnp.bfloat16):
    factor_of = level_of(rng, extent, pieces, -0.22, 0.18) if pieces else 1.0
    values = jax.random.normal(rng, extent, jnp.float32) * spread * factor_of
    return jnp.minimum(jnp.maximum(values, -most), most).astype(held_as)


def setup_inputs(seed: int = 0) -> dict:
    splits = jax.random.split(jax.random.key(seed), 11)
    return {
        "queue": scatter_about(splits[0], (TOKENS, D), 1.0, 6.0, ((0, 32), (1, 8))),
        "noise_block": scatter_about(splits[1], (TOK_CH, D), 1.0, 6.0, ((1, 8),)),
        "w_query": scatter_about(splits[2], (D, HEADS * HEAD_SIZE), D ** -0.5, 0.078125, ((0, 32), (1, 8))),
        "w_key": scatter_about(splits[3], (D, HEADS * HEAD_SIZE), D ** -0.5, 0.078125, ((0, 32), (1, 8))),
        "w_value": scatter_about(splits[4], (D, HEADS * HEAD_SIZE), D ** -0.5, 0.078125, ((0, 32), (1, 8))),
        "w_output": scatter_about(splits[5], (HEADS * HEAD_SIZE, D), (HEAD_SIZE // 8) ** -0.5, 1.5, ((0, 8), (1, 32))),
        "mod_table": scatter_about(splits[6], (LEVELS, 3, D), 1.0, 4.0, (), jnp.float32),
        "sigma_table": jnp.clip(jax.random.uniform(splits[7], (LEVELS + 1,), jnp.float32, 0.0, 1.0), 0.0, 1.0),
        "timestep_index": touch_ends(jax.random.randint(splits[8], (BLOCKS,), 0, LEVELS), jax.random.fold_in(splits[8], 1), 0, LEVELS - 1).astype(jnp.int32),
        "block_position": touch_ends(jax.random.randint(splits[9], (BLOCKS,), 0, 4096), jax.random.fold_in(splits[9], 1), 0, 4095).astype(jnp.int32),
    }


def norm_heads(vectors):
    return vectors * lax.rsqrt(lax.optimization_barrier(jnp.mean(vectors * vectors, axis=-1, keepdims=True)) + 1e-06)

def rotate(vectors, positions):
    half_size = vectors.shape[-1] // 2
    freqs = 10000.0 ** (-jnp.arange(half_size, dtype=jnp.float32) / half_size)
    angles = positions.astype(jnp.float32)[:, None] * freqs[None, :]
    cosine = jnp.cos(angles)[:, None, None, :]
    sine = jnp.sin(angles)[:, None, None, :]
    first = vectors[..., :half_size]
    second = vectors[..., half_size:]
    return jnp.concatenate([first * cosine - second * sine, first * sine + second * cosine], axis=-1)

def layer_step(queue_state, modulation, sigma_step, block_position, w_query, w_key, w_value, w_output):
    head_count = HEAD_DEV * N_HEAD
    wide_rows = queue_state.astype(jnp.float32).reshape(BLOCKS, TOK_CH, D)
    row_mean = lax.optimization_barrier(jnp.mean(wide_rows, axis=-1, keepdims=True))
    row_var = lax.optimization_barrier(jnp.mean((wide_rows - row_mean) ** 2, axis=-1, keepdims=True))
    normed = (wide_rows - row_mean) * lax.rsqrt(row_var + 1e-06)
    modulated = (normed * (1.0 + modulation[:, 1][:, None, :]) + modulation[:, 0][:, None, :]).astype(jnp.bfloat16).reshape(TOKENS, D)
    shape4 = (BLOCKS, TOK_CH, head_count, HEAD_SIZE)
    queries = rotate(norm_heads(jnp.dot(modulated, w_query, preferred_element_type=jnp.float32).reshape(shape4)), block_position).astype(jnp.bfloat16)
    key_rows = rotate(norm_heads(jnp.dot(modulated, w_key, preferred_element_type=jnp.float32).reshape(shape4)), block_position).astype(jnp.bfloat16)
    values = jnp.dot(modulated, w_value, preferred_element_type=jnp.float32).astype(jnp.bfloat16).reshape(shape4)
    padding = ((REACH, REACH), (0, 0), (0, 0), (0, 0))
    key_padded = jnp.pad(key_rows, padding)
    value_padded = jnp.pad(values, padding)
    span_blocks = 2 * REACH + 1

    def one_block(block):
        keys_near = lax.dynamic_slice_in_dim(key_padded, block, span_blocks, 0).reshape(span_blocks * TOK_CH, head_count, HEAD_SIZE).astype(jnp.float32)
        values_near = lax.dynamic_slice_in_dim(value_padded, block, span_blocks, 0).reshape(span_blocks * TOK_CH, head_count, HEAD_SIZE).astype(jnp.float32)
        near_block = block - REACH + jnp.arange(span_blocks * TOK_CH, dtype=jnp.int32) // TOK_CH
        allowed = (near_block >= 0) & (near_block < BLOCKS)
        query_here = lax.dynamic_index_in_dim(queries, block, 0, keepdims=False).astype(jnp.float32)
        scores = jnp.einsum('qhd,khd->hqk', query_here, keys_near) / math.sqrt(HEAD_SIZE)
        raised = jnp.where(allowed[None, None, :], jnp.exp(scores), 0.0)
        weights = (raised / lax.optimization_barrier(jnp.sum(raised, axis=-1, keepdims=True))).astype(jnp.bfloat16)
        attended = jnp.einsum('hqk,khd->qhd', weights.astype(jnp.float32), values_near)
        return attended.astype(jnp.bfloat16).reshape(TOK_CH, head_count * HEAD_SIZE)
    attended = lax.map(one_block, jnp.arange(BLOCKS, dtype=jnp.int32)).reshape(TOKENS, head_count * HEAD_SIZE)
    group_width = HEAD_DEV * HEAD_SIZE
    mixed_out = jnp.zeros((TOKENS, D), jnp.float32)
    for group_index in range(N_HEAD):
        lower = group_index * group_width
        product = jnp.dot(attended[:, lower:lower + group_width], w_output[lower:lower + group_width], preferred_element_type=jnp.float32)
        rounded = lax.optimization_barrier(product.astype(jnp.bfloat16))
        mixed_out = mixed_out + rounded.astype(jnp.float32)
    layer_out = wide_rows + modulation[:, 2][:, None, :] * mixed_out.reshape(BLOCKS, TOK_CH, D)
    following = wide_rows + sigma_step[:, None, None] * layer_out
    return (layer_out.astype(jnp.bfloat16).reshape(TOKENS, D), following.astype(jnp.bfloat16).reshape(TOKENS, D))

def reference(queue, noise_block, w_query, w_key, w_value, w_output, mod_table, sigma_table, timestep_index, block_position):
    modulation = mod_table[timestep_index]
    sigma_step = sigma_table[timestep_index + 1] - sigma_table[timestep_index]
    first_out, first_state = layer_step(queue, modulation, sigma_step, block_position, w_query, w_key, w_value, w_output)
    shifted = jnp.concatenate([first_state[TOK_CH:], noise_block], axis=0)
    velocity, queue_out = layer_step(shifted, modulation, sigma_step, block_position, w_query, w_key, w_value, w_output)
    return (velocity, queue_out)
```

```python
import functools
import math

import jax
import jax.numpy as jnp
from jax import lax
from jax.experimental import pallas as pl
from jax.experimental.pallas import tpu as pltpu
from jax.sharding import PartitionSpec as P

HEAD_SIZE = 128
NZ, NXH, NCORE = 8, 2, 2
NY, NXL = 4, 2
FRAMES = NZ * NXH * NCORE
HEADS_AXIS = NY * NXL
QK, QKV, INNER = 768, 1152, 384
SLAB = 160
CHUNK = 640
WIDTH = 5120
ROWS = 128
BLK = 64
F32 = jnp.float32
BF16 = jnp.bfloat16


def frame_of(z, xh, core):
    return ((z % NZ) * NXH + xh) * NCORE + core


def head_of(y, xl):
    return (y % NY) * NXL + xl


FRAME_COORDS = [(z, xh, c) for z in range(NZ) for xh in range(NXH) for c in range(NCORE)]
HEAD_COORDS = [(y, xl) for y in range(NY) for xl in range(NXL)]


def to_core(v):
    return lax.ppermute(
        v, "frame", [(frame_of(z, x, c), frame_of(z, x, 1 - c)) for z, x, c in FRAME_COORDS]
    )


def to_xh(v):
    return lax.ppermute(
        v, "frame", [(frame_of(z, x, c), frame_of(z, 1 - x, c)) for z, x, c in FRAME_COORDS]
    )


def along_z(v):
    return lax.ppermute(
        v,
        "frame",
        [(frame_of(z, x, c), frame_of(z + 1 - 2 * c, x, c)) for z, x, c in FRAME_COORDS],
    )


def to_xl(v):
    return lax.ppermute(v, "head", [(head_of(y, l), head_of(y, 1 - l)) for y, l in HEAD_COORDS])


def along_y(v, k):
    return lax.ppermute(v, "head", [(head_of(y, l), head_of(y + k, l)) for y, l in HEAD_COORDS])


def after(value, *others):
    return lax.optimization_barrier((value,) + others)[0]


def qkv_kernel(plan, n_pieces, ids, offs, *refs):
    xt = refs[0:4]
    xu = refs[4:6]
    modv, cosr, sinr = refs[6:9]
    pieces = refs[9 : 9 + n_pieces]
    q_out, kv_out = refs[9 + n_pieces : 11 + n_pieces]
    w, xm, sems = refs[11 + n_pieces :]

    groups = (384, 768, 0)
    copies = []
    slot = 0
    for low in groups:
        mine = []
        for piece, (rows, first, last) in zip(range(n_pieces), plan):
            if first <= low and low + INNER <= last:
                off = pl.multiple_of(offs[piece], 16)
                cp = pltpu.make_async_copy(
                    pieces[piece].at[:, pl.ds(low - first, INNER)],
                    w.at[pl.ds(off, rows), pl.ds(low, INNER)],
                    sems.at[slot],
                )
                cp.start()
                mine.append(cp)
                slot += 1
        copies.append(mine)

    y, xl = ids[0], ids[1]
    for b in range(2):
        spots = []
        for k in range(4):
            for r in range(2):
                j = lax.rem(y - k + NY, NY) * NXL + (xl + r - 2 * xl * r)
                if b == 0:
                    spots.append((j, xt[k], r * BLK))
                else:
                    spots.append((j, xu[r], k * BLK))

        def load(spot):
            return spot[1][spot[2] : spot[2] + BLK, :].astype(F32)

        def folded(v):
            t = v[:, 0:128]
            for i in range(1, 5):
                t = t + v[:, i * 128 : (i + 1) * 128]
            return t

        total = jnp.zeros((BLK, 128), F32)
        for s in spots:
            total = total + folded(load(s))
        mean = jnp.sum(total, axis=1, keepdims=True) * (1.0 / WIDTH)
        total = jnp.zeros((BLK, 128), F32)
        for s in spots:
            d = load(s) - mean
            total = total + folded(d * d)
        var = jnp.sum(total, axis=1, keepdims=True) * (1.0 / WIDTH)
        inv = lax.rsqrt(var + 1e-6)
        for s in spots:
            mv = modv[s[0]]
            v = (load(s) - mean) * inv
            v = v * (1.0 + mv[2 * b + 1 : 2 * b + 2, :]) + mv[2 * b : 2 * b + 1, :]
            col = pl.multiple_of(s[0] * CHUNK, 128)
            xm[b * BLK : (b + 1) * BLK, pl.ds(col, CHUNK)] = v.astype(BF16)

    def normed_rotated(acc, out, low):
        for h in range(3):
            v = acc[:, h * 128 : (h + 1) * 128]
            v = v * lax.rsqrt(jnp.mean(v * v, axis=1, keepdims=True) + 1e-6)
            turned = pltpu.roll(v, 64, 1)
            for b in range(2):
                rows = slice(b * BLK, (b + 1) * BLK)
                res = v[rows] * cosr[b : b + 1, :] + turned[rows] * sinr[b : b + 1, :]
                out[rows, low + h * 128 : low + (h + 1) * 128] = res.astype(BF16)

    for g, low in enumerate(groups):
        for cp in copies[g]:
            cp.wait()
        acc = jnp.dot(xm[...], w[:, low : low + INNER], preferred_element_type=F32)
        if low == 384:
            normed_rotated(acc, kv_out, 0)
        elif low == 768:
            kv_out[:, INNER:] = acc.astype(BF16)
        else:
            normed_rotated(acc, q_out, 0)


def project_qkv(ids, offs, plan, xt, xu, modv, cosr, sinr, pieces):
    n = len(pieces)
    n_copies = sum((last - first) // INNER for _, first, last in plan)
    vm = pl.BlockSpec(memory_space=pltpu.VMEM)
    sm = pl.BlockSpec(memory_space=pltpu.SMEM)
    return pl.pallas_call(
        functools.partial(qkv_kernel, plan, n),
        out_shape=(
            jax.ShapeDtypeStruct((ROWS, INNER), BF16),
            jax.ShapeDtypeStruct((ROWS, 2 * INNER), BF16),
        ),
        in_specs=[sm, sm] + [vm] * 9 + [pl.BlockSpec(memory_space=pl.ANY)] * n,
        out_specs=(vm, vm),
        scratch_shapes=[
            pltpu.VMEM((WIDTH, QKV), BF16),
            pltpu.VMEM((ROWS, WIDTH), BF16),
            pltpu.SemaphoreType.DMA((n_copies,)),
        ],
        compiler_params=pltpu.CompilerParams(vmem_limit_bytes=40 << 20),
        cost_estimate=pl.CostEstimate(
            flops=2 * ROWS * WIDTH * QKV, bytes_accessed=WIDTH * QKV * 2, transcendentals=0
        ),
    )(ids, offs, *xt, *xu, modv, cosr, sinr, *pieces)


def attn_kernel(plan, n_pieces, ids, offs, *refs):
    q, kv, kvl, kvr = refs[0:4]
    pieces = refs[4 : 4 + n_pieces]
    out = refs[4 + n_pieces]
    wo, att, sems = refs[5 + n_pieces :]
    copies = []
    for i, rows in enumerate(plan):
        off = pl.multiple_of(offs[i], 16)
        cp = pltpu.make_async_copy(pieces[i], wo.at[pl.ds(off, rows), :], sems.at[i])
        cp.start()
        copies.append(cp)
    row = lax.broadcasted_iota(jnp.int32, (ROWS, ROWS), 0)
    col = lax.broadcasted_iota(jnp.int32, (ROWS, ROWS), 1)
    ok_left = ((row < BLK) | (col >= BLK)) & (ids[2] > 0)
    ok_right = ((row >= BLK) | (col < BLK)) & (ids[2] < FRAMES - 1)
    nt = (((1,), (1,)), ((), ()))
    for h in range(3):
        lanes = slice(h * 128, (h + 1) * 128)
        vlanes = slice(INNER + h * 128, INNER + (h + 1) * 128)
        qh = q[:, lanes]
        es = []
        for ref, ok in ((kvl, ok_left), (kv, None), (kvr, ok_right)):
            s = lax.dot_general(qh, ref[:, lanes], nt, preferred_element_type=F32)
            e = jnp.exp(s * (1.0 / math.sqrt(HEAD_SIZE)))
            es.append(e if ok is None else jnp.where(ok, e, 0.0))
        total = jnp.sum(es[0] + es[1] + es[2], axis=1, keepdims=True)
        acc = jnp.zeros((ROWS, HEAD_SIZE), F32)
        for e, ref in zip(es, (kvl, kv, kvr)):
            acc = acc + jnp.dot(
                (e / total).astype(BF16), ref[:, vlanes], preferred_element_type=F32
            )
        att[:, lanes] = acc.astype(BF16)
    for cp in copies:
        cp.wait()
    a = att[...]
    for j in range(HEADS_AXIS):
        prod = lax.dot_general(
            a, wo[j * CHUNK : (j + 1) * CHUNK, :], nt, preferred_element_type=F32
        )
        out[j] = prod.astype(BF16)


def attend_project(ids, offs, plan, q, kv, kvl, kvr, pieces):
    n = len(pieces)
    vm = pl.BlockSpec(memory_space=pltpu.VMEM)
    sm = pl.BlockSpec(memory_space=pltpu.SMEM)
    return pl.pallas_call(
        functools.partial(attn_kernel, plan, n),
        out_shape=jax.ShapeDtypeStruct((HEADS_AXIS, ROWS, CHUNK), BF16),
        in_specs=[sm, sm] + [vm] * 4 + [pl.BlockSpec(memory_space=pl.ANY)] * n,
        out_specs=vm,
        scratch_shapes=[
            pltpu.VMEM((WIDTH, INNER), BF16),
            pltpu.VMEM((ROWS, INNER), BF16),
            pltpu.SemaphoreType.DMA((n,)),
        ],
        compiler_params=pltpu.CompilerParams(vmem_limit_bytes=24 << 20),
        cost_estimate=pl.CostEstimate(
            flops=2 * ROWS * WIDTH * INNER, bytes_accessed=WIDTH * INNER * 2, transcendentals=0
        ),
    )(ids, offs, q, kv, kvl, kvr, *pieces)


def per_device(
    queue,
    noise_block,
    w_query,
    w_key,
    w_value,
    w_output,
    mod_table,
    sigma_table,
    timestep_index,
    block_position,
):
    frame = lax.axis_index("frame")
    head = lax.axis_index("head")
    z, xh, core = frame // 4, (frame // 2) % 2, frame % 2
    y, xl = head // 2, head % 2
    ids = jnp.stack([y, xl, frame]).astype(jnp.int32)

    def pair(own, other, which):
        low = jnp.where(which == 0, own, other)
        high = jnp.where(which == 0, other, own)
        return jnp.concatenate([low, high], axis=0)

    def spread(a, b):
        ax = to_xl(a)
        bs = [b] + [along_y(b, k) for k in (1, 2, 3)]
        t = jnp.concatenate([a, ax], axis=0)
        ts = [t] + [along_y(t, k) for k in (1, 2, 3)]
        u = jnp.concatenate(bs, axis=0)
        return ts, [u, to_xl(u)]

    w = jnp.concatenate([w_query, w_key, w_value], axis=1)
    wo = w_output.T
    up = core == 0
    near = lambda d: jnp.where(up, z - d, z + d) % NZ
    far = lambda d: jnp.where(up, z + d, z - d) % NZ
    row_at = lambda zz, x, c: (zz * NXH + x) * 2 * SLAB + c * SLAB
    pieces, plan, offs = [], [], []

    def add(piece, first, last, off):
        pieces.append(piece)
        plan.append((piece.shape[0], first, last))
        offs.append(off)

    cw = to_core(w)
    xs = to_xh(w[:, :QK])
    one = pair(w, cw, core)
    add(one, 0, QKV, row_at(z, xh, 0))
    ts, us = spread(queue[:BLK], queue[BLK:])
    two = pair(xs, to_core(xs), core)
    add(two, 0, QK, row_at(z, 1 - xh, 0))
    xv = to_xh(w[:, QK:])
    cxv = to_core(xv)
    add(xv, QK, QKV, row_at(z, 1 - xh, core))
    add(cxv, QK, QKV, row_at(z, 1 - xh, 1 - core))
    held = [xv, cxv]
    for d in range(1, 5):
        if d == 4:
            one = jnp.where(up, one[:SLAB], one[SLAB:])
            two = jnp.where(up, two[:SLAB], two[SLAB:])
        one = along_z(after(one, *held))
        two = along_z(two)
        xv = to_xh(one[:, QK:])
        cone, ctwo, cxv = to_core(one), to_core(two), to_core(xv)
        held = [xv, cone, ctwo, cxv] if d < 3 else []
        own_core = 0 if d < 4 else core
        other_core = 0 if d < 4 else 1 - core
        add(one, 0, QKV, row_at(near(d), xh, own_core))
        add(cone, 0, QKV, row_at(far(d), xh, other_core))
        add(two, 0, QK, row_at(near(d), 1 - xh, own_core))
        add(ctwo, 0, QK, row_at(far(d), 1 - xh, other_core))
        add(xv, QK, QKV, row_at(near(d), 1 - xh, own_core))
        add(cxv, QK, QKV, row_at(far(d), 1 - xh, other_core))
    offs = jnp.stack(offs).astype(jnp.int32)

    opieces, oplan, ooffs = [], [], []

    def oadd(piece, off):
        opieces.append(piece)
        oplan.append(piece.shape[0])
        ooffs.append(off)

    owo = jnp.stack([wo, to_xh(wo)])
    cwo = to_core(owo)
    by_core = jnp.stack([jnp.where(up, owo, cwo), jnp.where(up, cwo, owo)], axis=1)
    obl = jnp.where(xh == 0, by_core, by_core[::-1]).reshape(4 * SLAB, INNER)
    oadd(obl, row_at(z, 0, 0))
    obl = after(obl, one, two)
    for d in range(1, 5):
        if d == 4:
            obl = jnp.where(up, obl[: 2 * SLAB], obl[2 * SLAB :])
        obl = along_z(obl)
        oadd(obl, row_at(near(d), 0 if d < 4 else core, 0))
        oadd(to_core(obl), row_at(far(d), 0 if d < 4 else 1 - core, 0))
    ooffs = jnp.stack(ooffs).astype(jnp.int32)

    rows = jnp.stack(
        [lax.dynamic_index_in_dim(mod_table, timestep_index[b], 0, False) for b in range(2)]
    )
    modv = rows[:, :2].reshape(4, HEADS_AXIS, CHUNK).transpose(1, 0, 2)
    gate = lax.dynamic_slice_in_dim(rows[:, 2], head * CHUNK, CHUNK, 1)
    table_index = jnp.arange(sigma_table.shape[0], dtype=jnp.int32)[None, :]
    pick = lambda index: jnp.sum(
        jnp.where(index[:, None] == table_index, sigma_table[None, :], 0.0), axis=1
    )
    sigma_step = pick(timestep_index + 1) - pick(timestep_index)
    half = HEAD_SIZE // 2
    freqs = 10000.0 ** (-jnp.arange(half, dtype=F32) / half)
    angles = block_position.astype(F32)[:, None] * freqs[None, :]
    cosr = jnp.concatenate([jnp.cos(angles), jnp.cos(angles)], axis=1)
    sinr = jnp.concatenate([-jnp.sin(angles), jnp.sin(angles)], axis=1)

    def mixed_of(ts, us):
        q, kv = project_qkv(ids, offs, tuple(plan), ts, us, modv, cosr, sinr, pieces)
        kvl = lax.ppermute(kv, "frame", [(i, i + 1) for i in range(FRAMES - 1)])
        kvr = lax.ppermute(kv, "frame", [(i + 1, i) for i in range(FRAMES - 1)])
        prod = attend_project(ids, ooffs, tuple(oplan), q, kv, kvl, kvr, opieces)
        got = lax.all_to_all(
            prod.reshape(HEADS_AXIS * ROWS, CHUNK), "head", 0, 0, tiled=True
        ).reshape(HEADS_AXIS, ROWS, CHUNK)
        return jnp.sum(got.astype(F32), axis=0)

    def advance(base, mixed):
        wide = base.astype(F32).reshape(2, BLK, CHUNK)
        layer_out = wide + gate[:, None, :] * mixed.reshape(2, BLK, CHUNK)
        following = wide + sigma_step[:, None, None] * layer_out
        return (
            layer_out.astype(BF16).reshape(ROWS, CHUNK),
            following.astype(BF16).reshape(ROWS, CHUNK),
        )

    _, state = advance(queue, mixed_of(ts, us))
    moved_in = lax.ppermute(state[:BLK], "frame", [(i + 1, i) for i in range(FRAMES - 1)])
    entering = jnp.where(frame == FRAMES - 1, noise_block, moved_in)
    second = jnp.concatenate([state[BLK:], entering], axis=0)
    return advance(second, mixed_of(*spread(state[BLK:], entering)))


def solution(mesh):
    in_specs = (
        P("frame", "head"),
        P(None, "head"),
        P("frame", "head"),
        P("frame", "head"),
        P("frame", "head"),
        P("head", "frame"),
        P(),
        P(),
        P("frame"),
        P("frame"),
    )
    out_specs = (P("frame", "head"), P("frame", "head"))
    return jax.shard_map(
        per_device, mesh=mesh, in_specs=in_specs, out_specs=out_specs, check_vma=False
    )
```

```python
import functools
import math

import jax
import jax.numpy as jnp
from jax import lax
from jax.experimental import pallas as pl
from jax.experimental.pallas import tpu as pltpu
from jax.sharding import PartitionSpec as P

HEAD_SIZE = 128
NZ, NXH, NCORE = 8, 2, 2
NY, NXL = 4, 2
FRAMES = NZ * NXH * NCORE
HEADS_AXIS = NY * NXL
INNER = 384
SLAB, PART = 160, 80
HALF = 3 * SLAB + PART
CHUNK = 640
WIDTH = 5120
ROWS = 128
BLK = 64
F32 = jnp.float32
BF16 = jnp.bfloat16


def frame_of(z, xh, core):
    return ((z % NZ) * NXH + xh) * NCORE + core


def head_of(y, xl):
    return (y % NY) * NXL + xl


FRAME_COORDS = [(z, xh, c) for z in range(NZ) for xh in range(NXH) for c in range(NCORE)]
HEAD_COORDS = [(y, xl) for y in range(NY) for xl in range(NXL)]


def to_core(v):
    return lax.ppermute(
        v, "frame", [(frame_of(z, x, c), frame_of(z, x, 1 - c)) for z, x, c in FRAME_COORDS]
    )


def to_xh(v):
    return lax.ppermute(
        v, "frame", [(frame_of(z, x, c), frame_of(z, 1 - x, c)) for z, x, c in FRAME_COORDS]
    )


def along_z(v):
    return lax.ppermute(
        v,
        "frame",
        [(frame_of(z, x, c), frame_of(z + 1 - 2 * c, x, c)) for z, x, c in FRAME_COORDS],
    )


def to_bound(v):
    pairs = [(i, i + 1) for i in range(1, FRAMES - 1, 2)]
    return lax.ppermute(v, "frame", pairs + [(j, i) for i, j in pairs])


def to_xl(v):
    return lax.ppermute(v, "head", [(head_of(y, l), head_of(y, 1 - l)) for y, l in HEAD_COORDS])


def along_y(v, k):
    return lax.ppermute(v, "head", [(head_of(y, l), head_of(y + k, l)) for y, l in HEAD_COORDS])


def after(value, *others):
    return lax.optimization_barrier((value,) + others)[0]


def normed_rotated(acc, cosr, sinr, out):
    for h in range(3):
        v = acc[:, h * 128 : (h + 1) * 128]
        v = v * lax.rsqrt(jnp.mean(v * v, axis=1, keepdims=True) + 1e-6)
        turned = pltpu.roll(v, 64, 1)
        for b in range(2):
            rows = slice(b * BLK, (b + 1) * BLK)
            res = v[rows] * cosr[b : b + 1, :] + turned[rows] * sinr[b : b + 1, :]
            out[rows, h * 128 : (h + 1) * 128] = res.astype(BF16)


def fetch(plan, offs, pieces, shift, dst, sems, slot):
    copies = []
    for i, (piece, low, rows) in enumerate(plan):
        cp = pltpu.make_async_copy(
            pieces[piece].at[pl.ds(low + shift, rows), :],
            dst.at[pl.ds(pl.multiple_of(offs[i], 16), rows), :],
            sems.at[slot + i],
        )
        cp.start()
        copies.append(cp)
    return copies


def q_kernel(plan, n_pieces, offs, xm, cosr, sinr, *refs):
    pieces = refs[:n_pieces]
    q_out, w, sems = refs[n_pieces:]
    for cp in fetch(plan, offs, pieces, 0, w, sems, 0):
        cp.wait()
    acc = jnp.dot(xm[...], w[...], preferred_element_type=F32)
    normed_rotated(acc, cosr, sinr, q_out)


def kv_kernel(plan, n_pieces, n_x, ids, offs, steps, *refs):
    xs = refs[0:n_x]
    table, cosr, sinr = refs[n_x : n_x + 3]
    refs = refs[n_x + 3 :]
    pieces = refs[0:n_pieces]
    kv_out, xm = refs[n_pieces : n_pieces + 2]
    w_key, w_value, modv, mod_sems, sems = refs[n_pieces + 2 :]

    mods = []
    for b in range(2):
        eight = pl.ds(pl.multiple_of(steps[b] // 8 * 8, 8), 8)
        cp = pltpu.make_async_copy(table.at[0:2, eight, :], modv.at[b], mod_sems.at[b])
        cp.start()
        mods.append(cp)

    key_copies = fetch(plan, offs, pieces, SLAB, w_key, sems, 0)
    value_copies = fetch(plan, offs, pieces, 2 * SLAB, w_value, sems, len(plan))

    y, xl = ids[0], ids[1]
    for b in range(2):
        spots = []
        for k in range(4):
            for r in range(2):
                j = lax.rem(y - k + NY, NY) * NXL + (xl + r - 2 * xl * r)
                if n_x == 1:
                    j = 2 * k + r
                    spots.append((j, xs[0], j * ROWS + b * BLK))
                elif b == 0:
                    spots.append((j, xs[k], r * BLK))
                else:
                    spots.append((j, xs[4 + r], k * BLK))

        def load(spot):
            return spot[1][spot[2] : spot[2] + BLK, :].astype(F32)

        def folded(v):
            t = v[:, 0:128]
            for i in range(1, 5):
                t = t + v[:, i * 128 : (i + 1) * 128]
            return t

        total = jnp.zeros((BLK, 128), F32)
        for s in spots:
            total = total + folded(load(s))
        mean = jnp.sum(total, axis=1, keepdims=True) * (1.0 / WIDTH)
        total = jnp.zeros((BLK, 128), F32)
        for s in spots:
            d = load(s) - mean
            total = total + folded(d * d)
        var = jnp.sum(total, axis=1, keepdims=True) * (1.0 / WIDTH)
        inv = lax.rsqrt(var + 1e-6)
        mods[b].wait()
        for s in spots:
            col = s[0] * CHUNK if n_x == 1 else pl.multiple_of(s[0] * CHUNK, 128)
            cols = pl.ds(col, CHUNK)
            row = pl.ds(lax.rem(steps[b], 8), 1)
            v = (load(s) - mean) * inv
            v = v * (1.0 + modv[b, 1, row, cols]) + modv[b, 0, row, cols]
            xm[b * BLK : (b + 1) * BLK, cols] = v.astype(BF16)

    for cp in key_copies:
        cp.wait()
    acc = jnp.dot(xm[...], w_key[...], preferred_element_type=F32)
    normed_rotated(acc, cosr, sinr, kv_out)
    for cp in value_copies:
        cp.wait()
    acc = jnp.dot(xm[...], w_value[...], preferred_element_type=F32)
    kv_out[:, INNER:] = acc.astype(BF16)


def project_kv(ids, offs, steps, plan, xs, table, cosr, sinr, pieces):
    n = len(pieces)
    hbm = pl.BlockSpec(memory_space=pltpu.HBM)
    vm = pl.BlockSpec(memory_space=pltpu.VMEM)
    sm = pl.BlockSpec(memory_space=pltpu.SMEM)
    return pl.pallas_call(
        functools.partial(kv_kernel, plan, n, len(xs)),
        out_shape=(
            jax.ShapeDtypeStruct((ROWS, 2 * INNER), BF16),
            jax.ShapeDtypeStruct((ROWS, WIDTH), BF16),
        ),
        in_specs=[sm] * 3 + [vm] * len(xs) + [hbm, vm, vm] + [hbm] * n,
        out_specs=(vm, vm),
        scratch_shapes=[
            pltpu.VMEM((WIDTH, INNER), BF16),
            pltpu.VMEM((WIDTH, INNER), BF16),
            pltpu.VMEM((2, 2, 8, WIDTH), F32),
            pltpu.SemaphoreType.DMA((2,)),
            pltpu.SemaphoreType.DMA((2 * len(plan),)),
        ],
        compiler_params=pltpu.CompilerParams(vmem_limit_bytes=60 << 20),
        cost_estimate=pl.CostEstimate(
            flops=4 * ROWS * WIDTH * INNER, bytes_accessed=WIDTH * INNER * 4, transcendentals=0
        ),
    )(ids, offs, steps, *xs, table, cosr, sinr, *pieces)


def project_q(offs, plan, xm, cosr, sinr, pieces):
    n = len(pieces)
    hbm = pl.BlockSpec(memory_space=pltpu.HBM)
    vm = pl.BlockSpec(memory_space=pltpu.VMEM)
    return pl.pallas_call(
        functools.partial(q_kernel, plan, n),
        out_shape=jax.ShapeDtypeStruct((ROWS, INNER), BF16),
        in_specs=[pl.BlockSpec(memory_space=pltpu.SMEM), vm, vm, vm] + [hbm] * n,
        out_specs=vm,
        scratch_shapes=[pltpu.VMEM((WIDTH, INNER), BF16), pltpu.SemaphoreType.DMA((len(plan),))],
        compiler_params=pltpu.CompilerParams(vmem_limit_bytes=60 << 20),
        cost_estimate=pl.CostEstimate(
            flops=2 * ROWS * WIDTH * INNER, bytes_accessed=WIDTH * INNER * 2, transcendentals=0
        ),
    )(offs, xm, cosr, sinr, *pieces)


def banded(ids, q, kv, kvc, kvb, att):
    row = lax.broadcasted_iota(jnp.int32, (ROWS, ROWS), 0)
    col = lax.broadcasted_iota(jnp.int32, (ROWS, ROWS), 1)
    core = ids[3]
    on_left = (row < BLK) | (col >= BLK)
    on_right = (row >= BLK) | (col < BLK)
    ok_c = (on_left & (core == 1)) | (on_right & (core == 0))
    inside = (ids[2] > 0) & (ids[2] < FRAMES - 1)
    ok_b = ((on_left & (core == 0)) | (on_right & (core == 1))) & inside
    nt = (((1,), (1,)), ((), ()))
    for h in range(3):
        lanes = slice(h * 128, (h + 1) * 128)
        vlanes = slice(INNER + h * 128, INNER + (h + 1) * 128)
        qh = q[:, lanes]
        es = []
        for ref, ok in ((kvc, ok_c), (kv, None), (kvb, ok_b)):
            s = lax.dot_general(qh, ref[:, lanes], nt, preferred_element_type=F32)
            e = jnp.exp(s * (1.0 / math.sqrt(HEAD_SIZE)))
            es.append(e if ok is None else jnp.where(ok, e, 0.0))
        total = jnp.sum(es[0] + es[1] + es[2], axis=1, keepdims=True)
        acc = jnp.zeros((ROWS, HEAD_SIZE), F32)
        for e, ref in zip(es, (kvc, kv, kvb)):
            acc = acc + jnp.dot(
                (e / total).astype(BF16), ref[:, vlanes], preferred_element_type=F32
            )
        att[:, lanes] = acc.astype(BF16)


def attn_kernel(ids, q, kv, kvc, kvb, att):
    banded(ids, q, kv, kvc, kvb, att)


def out_kernel(plan, n_pieces, with_attention, ids, offs, *refs):
    n_in = 4 if with_attention else 1
    pieces = refs[n_in : n_in + n_pieces]
    out, wo, att, sems = refs[n_in + n_pieces :]
    copies = fetch(plan, offs, pieces, 0, wo, sems, 0)
    if with_attention:
        banded(ids, *refs[:4], att)
        a = att[...]
    else:
        a = refs[0][...]
    for cp in copies:
        cp.wait()
    nt = (((1,), (1,)), ((), ()))
    for j in range(HEADS_AXIS):
        prod = lax.dot_general(
            a, wo[j * CHUNK : (j + 1) * CHUNK, :], nt, preferred_element_type=F32
        )
        out[j] = prod.astype(BF16)


def attend(ids, q, kv, kvc, kvb):
    vm = pl.BlockSpec(memory_space=pltpu.VMEM)
    sm = pl.BlockSpec(memory_space=pltpu.SMEM)
    return pl.pallas_call(
        attn_kernel,
        out_shape=jax.ShapeDtypeStruct((ROWS, INNER), BF16),
        in_specs=[sm] + [vm] * 4,
        out_specs=vm,
        compiler_params=pltpu.CompilerParams(vmem_limit_bytes=60 << 20),
        cost_estimate=pl.CostEstimate(
            flops=12 * ROWS * ROWS * INNER, bytes_accessed=ROWS * INNER * 8, transcendentals=0
        ),
    )(ids, q, kv, kvc, kvb)


def project_out(ids, offs, plan, ins, pieces):
    n = len(pieces)
    vm = pl.BlockSpec(memory_space=pltpu.VMEM)
    sm = pl.BlockSpec(memory_space=pltpu.SMEM)
    return pl.pallas_call(
        functools.partial(out_kernel, plan, n, len(ins) == 4),
        out_shape=jax.ShapeDtypeStruct((HEADS_AXIS, ROWS, CHUNK), BF16),
        in_specs=[sm, sm] + [vm] * len(ins) + [pl.BlockSpec(memory_space=pltpu.HBM)] * n,
        out_specs=vm,
        scratch_shapes=[
            pltpu.VMEM((WIDTH, INNER), BF16),
            pltpu.VMEM((ROWS, INNER), BF16),
            pltpu.SemaphoreType.DMA((len(plan),)),
        ],
        compiler_params=pltpu.CompilerParams(vmem_limit_bytes=60 << 20),
        cost_estimate=pl.CostEstimate(
            flops=2 * ROWS * WIDTH * INNER, bytes_accessed=WIDTH * INNER * 2, transcendentals=0
        ),
    )(ids, offs, *ins, *pieces)


def join_kernel(wq, wk, wv, wo, out):
    for i, ref in enumerate((wq, wk, wv, wo)):
        out[i * SLAB : (i + 1) * SLAB, :] = ref[...]


def joined(wq, wk, wv, wo):
    return pl.pallas_call(
        join_kernel,
        out_shape=jax.ShapeDtypeStruct((4 * SLAB, INNER), BF16),
        compiler_params=pltpu.CompilerParams(vmem_limit_bytes=60 << 20),
    )(wq, wk, wv, wo)


def update_kernel(first, ids, steps, sigma, table, got, base0, base1, *refs):
    if first:
        noise, out0, out1, gate, sems = refs
    else:
        out0, out1, gate, sems = refs
    copies = []
    for b in range(2):
        cols = pl.ds(pl.multiple_of(ids[4] * CHUNK, 128), CHUNK)
        eight = pl.ds(pl.multiple_of(steps[b] // 8 * 8, 8), 8)
        cp = pltpu.make_async_copy(table.at[2, eight, cols], gate.at[b], sems.at[b])
        cp.start()
        copies.append(cp)
    for b, base in enumerate((base0, base1)):
        rows = slice(b * BLK, (b + 1) * BLK)
        mixed = got[0, rows, :].astype(F32)
        for j in range(1, HEADS_AXIS):
            mixed = mixed + got[j, rows, :].astype(F32)
        copies[b].wait()
        wide = base[...].astype(F32)
        layer_out = wide + gate[b, pl.ds(lax.rem(steps[b], 8), 1), :] * mixed
        t = steps[b]
        following = wide + (sigma[t + 1] - sigma[t]) * layer_out
        if not first:
            out0[rows, :] = layer_out.astype(BF16)
            out1[rows, :] = following.astype(BF16)
        elif b == 0:
            out0[...] = jnp.where(ids[2] == 0, noise[...], following.astype(BF16))
        else:
            out1[...] = following.astype(BF16)


def update(ids, steps, sigma, table, got, base0, base1, *noise):
    first = len(noise) == 1
    vm = pl.BlockSpec(memory_space=pltpu.VMEM)
    sm = pl.BlockSpec(memory_space=pltpu.SMEM)
    hbm = pl.BlockSpec(memory_space=pltpu.HBM)
    shape = (BLK if first else ROWS, CHUNK)
    return pl.pallas_call(
        functools.partial(update_kernel, first),
        out_shape=(jax.ShapeDtypeStruct(shape, BF16),) * 2,
        in_specs=[sm, sm, sm, hbm] + [vm] * (3 + len(noise)),
        out_specs=(vm, vm),
        scratch_shapes=[pltpu.VMEM((2, 8, CHUNK), F32), pltpu.SemaphoreType.DMA((2,))],
        compiler_params=pltpu.CompilerParams(vmem_limit_bytes=60 << 20),
    )(ids, steps, sigma, table, got, base0, base1, *noise)


def per_device(
    queue,
    noise_block,
    w_query,
    w_key,
    w_value,
    w_output,
    mod_table,
    sigma_table,
    timestep_index,
    block_position,
):
    frame = lax.axis_index("frame")
    head = lax.axis_index("head")
    z, xh, core = frame // 4, (frame // 2) % 2, frame % 2
    y, xl = head // 2, head % 2
    ids = jnp.stack([y, xl, frame, core, head]).astype(jnp.int32)
    table = mod_table.transpose(1, 0, 2)
    half = HEAD_SIZE // 2
    freqs = 10000.0 ** (-jnp.arange(half, dtype=F32) / half)
    angles = block_position.astype(F32)[:, None] * freqs[None, :]
    cosr = jnp.concatenate([jnp.cos(angles), jnp.cos(angles)], axis=1)
    sinr = jnp.concatenate([-jnp.sin(angles), jnp.sin(angles)], axis=1)

    up = core == 0
    near = lambda d: jnp.where(up, z - d, z + d) % NZ
    far = lambda d: jnp.where(up, z + d, z - d) % NZ
    row_at = lambda zz, x, c: (zz * NXH + x) * 2 * SLAB + c * SLAB
    w = joined(w_query, w_key, w_value, w_output.T)
    cw = to_core(w)
    low, high = jnp.where(up, w, cw), jnp.where(up, cw, w)
    cut = lambda v: (v[: 3 * SLAB], v[3 * SLAB : 3 * SLAB + PART], v[3 * SLAB + PART :])
    (low, low_a, low_b), (high, high_a, high_b) = cut(low), cut(high)
    h1 = [jnp.concatenate([low, low_a, high, low_b], axis=0)]
    h1.append(along_z(h1[0]))
    xs = to_xh(after(w[: 3 * SLAB], cw))
    cxs = to_core(after(xs, h1[1]))
    low, high = jnp.where(up, xs, cxs), jnp.where(up, cxs, xs)
    h2 = [jnp.concatenate([low, high_a, high, high_b], axis=0)]
    h2.append(along_z(h2[0]))
    copies = jnp.broadcast_to(after(queue, cxs)[None], (HEADS_AXIS, ROWS, CHUNK))
    whole = lax.all_to_all(copies.reshape(-1, CHUNK), "head", 0, 0, tiled=True)

    qkv_at = [row_at(z, x, c) for x in (xh, 1 - xh) for c in (0, 1)]
    out_at = [row_at(z, xh, c) + e for c in (0, 1) for e in (0, PART)]
    both = ((near, core), (far, 1 - core))
    for d in range(1, 4):
        for x in (xh, 1 - xh):
            for side, c in both:
                first = c if d == 3 and x is not xh else 0
                qkv_at += [row_at(side(d), x, first), row_at(side(d), x, 1 - first)]
        for half in (0, 1):
            for side, c in both:
                first = c if d == 3 and half == 1 else 0
                out_at += [row_at(side(d), xh, half) + e * PART for e in (first, 1 - first)]
    for x in (xh, 1 - xh):
        qkv_at += [row_at(near(4), x, c) for c in (core, 1 - core)]
    for half in (0, 1):
        out_at += [row_at(near(4), xh, half) + e * PART for e in (core, 1 - core)]
    for side, c in both:
        out_at.append(row_at(z, 1 - xh, c))
        out_at += [row_at(side(d), 1 - xh, 0) for d in (1, 2)]
    for side, c in both:
        out_at.append(row_at(side(3), 1 - xh, 0))
        out_at += [row_at(side(3), 1 - xh, 1) + e * PART for e in (c, 1 - c)]
        out_at += [row_at(near(4), 1 - xh, half) + c * PART for half in (0, 1)]
    qkv_spots = jnp.stack(qkv_at).astype(jnp.int32)
    out_spots = jnp.stack(out_at).astype(jnp.int32)

    mine = lambda v: jnp.where(up, v[:HALF], v[HALF:])
    other = lambda v: jnp.where(up, v[HALF:], v[:HALF])
    out_rows = lambda v: [v[3 * SLAB : HALF], v[HALF + 3 * SLAB :]]
    h1.append(along_z(h1[1]))
    h2.append(along_z(h2[1]))
    c1 = [to_core(h1[1])]
    c2 = [to_core(h2[1])]
    c1.append(to_core(after(h1[2], c1[0])))
    c2.append(to_core(after(h2[2], c2[0])))
    h1.append(along_z(after(h1[2], c1[0])))
    gated = after(h2[2], c2[0], ids, cosr, sinr, qkv_spots, out_spots, whole)
    h2.append(along_z(mine(gated)))
    rest = along_z(other(gated))
    parts = [w[3 * SLAB :]]
    for d in (1, 2):
        parts += out_rows(h1[d]) + out_rows(h2[d])
    x_out = to_xh(jnp.concatenate(parts, axis=0))
    c1.append(to_core(after(h1[3], c1[1])))
    h1.append(along_z(after(mine(h1[3]), c1[1])))
    h2.append(along_z(after(h2[3], c2[1])))
    c1.append(to_core(after(h1[4], c1[2])))
    c2.append(to_core(after(h2[3], c1[2])))
    c_rest = to_core(after(rest, c2[2]))
    c2.append(to_core(after(h2[4], c_rest)))
    parts = out_rows(h1[3])
    parts += [h[3 * SLAB :] for h in (h2[3], rest, h1[4], h2[4])]
    x_end = to_xh(jnp.concatenate(parts, axis=0))

    pieces = [h1[0], h2[0], h1[1], c1[0], h2[1], c2[0], h1[2], c1[1], h2[2], c2[1]]
    pieces += [h1[3], c1[2], h2[3], rest, c2[2], c_rest, h1[4], c1[3], h2[4], c2[3]]
    plan, out_plan = [], []
    for i, piece in enumerate(pieces):
        for row in range(0, piece.shape[0], HALF):
            plan.append((i, row, SLAB))
            out_plan.append((i, row + 3 * SLAB, PART))
    n = len(pieces)
    for i in (n, n + 1):
        out_plan += [(i, 0, SLAB), (i, SLAB, 2 * SLAB), (i, 3 * SLAB, 2 * SLAB)]
    for i in (n + 2, n + 3):
        out_plan += [(i, 0, SLAB)] + [(i, SLAB + e * PART, PART) for e in range(4)]
    plan, out_plan = tuple(plan), tuple(out_plan)

    def projected(xs):
        kv, xm = project_kv(
            ids, qkv_spots, timestep_index, plan, xs, table, cosr, sinr, pieces
        )
        kvb = to_bound(kv)
        kvc = to_core(kv)
        q = project_q(qkv_spots, plan, xm, cosr, sinr, pieces)
        return q, kv, kvc, kvb

    def mixed_of(q, kv, kvc, kvb, out_pieces):
        prod = project_out(ids, out_spots, out_plan, [q, kv, kvc, kvb], out_pieces)
        return lax.all_to_all(
            prod.reshape(HEADS_AXIS * ROWS, CHUNK), "head", 0, 0, tiled=True
        ).reshape(HEADS_AXIS, ROWS, CHUNK)

    q, kv, kvc, kvb = projected([whole])
    cx_out = to_core(after(x_out, kv))
    cx_end = to_core(after(x_end, kv))
    out_pieces = pieces + [x_out, cx_out, x_end, cx_end]
    got = mixed_of(q, kv, kvc, kvb, out_pieces)
    leaving, a = update(
        ids, timestep_index, sigma_table, table, got, queue[:BLK], queue[BLK:], noise_block
    )

    def handed_back(v, k):
        perm = []
        for f in range(FRAMES):
            for yy, ll in HEAD_COORDS:
                perm.append(
                    (
                        f * HEADS_AXIS + head_of(yy, ll),
                        ((f - 1) % FRAMES) * HEADS_AXIS + head_of(yy + k, ll),
                    )
                )
        return lax.ppermute(v, ("frame", "head"), perm)

    ax = to_xl(a)
    bs = [handed_back(leaving, k) for k in range(4)]
    t = jnp.concatenate([a, ax], axis=0)
    ts = [t] + [along_y(t, k) for k in (1, 2, 3)]
    u = jnp.concatenate(bs, axis=0)
    got = mixed_of(*projected(ts + [u, to_xl(u)]), out_pieces)
    return update(ids, timestep_index, sigma_table, table, got, a, bs[0])


def solution(mesh):
    in_specs = (
        P("frame", "head"),
        P(None, "head"),
        P("frame", "head"),
        P("frame", "head"),
        P("frame", "head"),
        P("head", "frame"),
        P(),
        P(),
        P("frame"),
        P("frame"),
    )
    out_specs = (P("frame", "head"), P("frame", "head"))
    return jax.shard_map(
        per_device, mesh=mesh, in_specs=in_specs, out_specs=out_specs, check_vma=False
    )
```

```python
import functools
import math

import jax
import jax.numpy as jnp
from jax import lax
from jax.experimental import pallas as pl
from jax.experimental.pallas import tpu as pltpu
from jax.sharding import PartitionSpec as P

HEAD_SIZE = 128
NZ, NXH, NCORE = 8, 2, 2
NY, NXL = 4, 2
FRAMES = NZ * NXH * NCORE
HEADS_AXIS = NY * NXL
INNER = 384
SLAB, PART = 160, 80
HALF = 3 * SLAB + PART
CHUNK = 640
WIDTH = 5120
ROWS = 128
BLK = 64
F32 = jnp.float32
BF16 = jnp.bfloat16


def frame_of(z, xh, core):
    return ((z % NZ) * NXH + xh) * NCORE + core


def head_of(y, xl):
    return (y % NY) * NXL + xl


FRAME_COORDS = [(z, xh, c) for z in range(NZ) for xh in range(NXH) for c in range(NCORE)]
HEAD_COORDS = [(y, xl) for y in range(NY) for xl in range(NXL)]


def to_core(v):
    return lax.ppermute(
        v, "frame", [(frame_of(z, x, c), frame_of(z, x, 1 - c)) for z, x, c in FRAME_COORDS]
    )


def to_xh(v):
    return lax.ppermute(
        v, "frame", [(frame_of(z, x, c), frame_of(z, 1 - x, c)) for z, x, c in FRAME_COORDS]
    )


def along_z(v):
    return lax.ppermute(
        v,
        "frame",
        [(frame_of(z, x, c), frame_of(z + 1 - 2 * c, x, c)) for z, x, c in FRAME_COORDS],
    )


def to_bound(v):
    pairs = [(i, i + 1) for i in range(1, FRAMES - 1, 2)]
    return lax.ppermute(v, "frame", pairs + [(j, i) for i, j in pairs])


def to_xl(v):
    return lax.ppermute(v, "head", [(head_of(y, l), head_of(y, 1 - l)) for y, l in HEAD_COORDS])


def along_y(v, k):
    return lax.ppermute(v, "head", [(head_of(y, l), head_of(y + k, l)) for y, l in HEAD_COORDS])


def after(value, *others):
    return lax.optimization_barrier((value,) + others)[0]


def normed_rotated(acc, cosr, sinr, out):
    for h in range(3):
        v = acc[:, h * 128 : (h + 1) * 128]
        v = v * lax.rsqrt(jnp.mean(v * v, axis=1, keepdims=True) + 1e-6)
        turned = pltpu.roll(v, 64, 1)
        for b in range(2):
            rows = slice(b * BLK, (b + 1) * BLK)
            res = v[rows] * cosr[b : b + 1, :] + turned[rows] * sinr[b : b + 1, :]
            out[rows, h * 128 : (h + 1) * 128] = res.astype(BF16)


def fetch(plan, offs, pieces, shift, dst, sems, slot):
    copies = []
    for i, (piece, low, rows) in enumerate(plan):
        cp = pltpu.make_async_copy(
            pieces[piece].at[pl.ds(low + shift, rows), :],
            dst.at[pl.ds(pl.multiple_of(offs[i], 16), rows), :],
            sems.at[slot + i],
        )
        cp.start()
        copies.append(cp)
    return copies


def q_kernel(plan, n_pieces, offs, xm, cosr, sinr, *refs):
    pieces = refs[:n_pieces]
    q_out, w, sems = refs[n_pieces:]
    for cp in fetch(plan, offs, pieces, 0, w, sems, 0):
        cp.wait()
    acc = jnp.dot(xm[...], w[...], preferred_element_type=F32)
    normed_rotated(acc, cosr, sinr, q_out)


def start_modulation(steps, table, modv, mod_sems):
    mods = []
    for b in range(2):
        eight = pl.ds(pl.multiple_of(steps[b] // 8 * 8, 8), 8)
        cp = pltpu.make_async_copy(table.at[0:2, eight, :], modv.at[b], mod_sems.at[b])
        cp.start()
        mods.append(cp)
    return mods


def modulate(n_x, ids, steps, xs, mods, modv, xm):
    y, xl = ids[0], ids[1]
    for b in range(2):
        spots = []
        for k in range(4):
            for r in range(2):
                j = lax.rem(y - k + NY, NY) * NXL + (xl + r - 2 * xl * r)
                if n_x == 1:
                    j = 2 * k + r
                    spots.append((j, xs[0], j * ROWS + b * BLK))
                elif b == 0:
                    spots.append((j, xs[k], r * BLK))
                else:
                    spots.append((j, xs[4 + k], r * BLK))

        def load(spot):
            return spot[1][spot[2] : spot[2] + BLK, :].astype(F32)

        def folded(v):
            t = v[:, 0:128]
            for i in range(1, 5):
                t = t + v[:, i * 128 : (i + 1) * 128]
            return t

        total = jnp.zeros((BLK, 128), F32)
        for s in spots:
            total = total + folded(load(s))
        mean = jnp.sum(total, axis=1, keepdims=True) * (1.0 / WIDTH)
        total = jnp.zeros((BLK, 128), F32)
        for s in spots:
            d = load(s) - mean
            total = total + folded(d * d)
        var = jnp.sum(total, axis=1, keepdims=True) * (1.0 / WIDTH)
        inv = lax.rsqrt(var + 1e-6)
        mods[b].wait()
        for s in spots:
            col = s[0] * CHUNK if n_x == 1 else pl.multiple_of(s[0] * CHUNK, 128)
            cols = pl.ds(col, CHUNK)
            row = pl.ds(lax.rem(steps[b], 8), 1)
            v = (load(s) - mean) * inv
            v = v * (1.0 + modv[b, 1, row, cols]) + modv[b, 0, row, cols]
            xm[b * BLK : (b + 1) * BLK, cols] = v.astype(BF16)


def part_kernel(plan, slots, n_slots, n_pieces, first, last, offs, *refs):
    if first:
        ids, steps, whole, table = refs[:4]
        refs = refs[4:]
    else:
        xm, acc_in = refs[:2]
        refs = refs[2:]
        if last:
            cosr, sinr = refs[:2]
            refs = refs[2:]
    pieces = refs[:n_pieces]
    refs = refs[n_pieces:]
    if first:
        acc_out, xm, w, sems, modv, mod_sems = refs
        mods = start_modulation(steps, table, modv, mod_sems)
    elif last:
        q_out, kv_out, w, sems = refs
    else:
        acc_out, w, sems = refs
    copies = []
    for p in (1, 2, 0):
        for i, (piece, low, rows) in enumerate(plan):
            off = slots[i] * CHUNK + lax.rem(offs[i], CHUNK)
            cp = pltpu.make_async_copy(
                pieces[piece].at[pl.ds(low + p * SLAB, rows), :],
                w.at[p, pl.ds(pl.multiple_of(off, 16), rows), :],
                sems.at[p * len(plan) + i],
            )
            cp.start()
            copies.append(cp)
    if first:
        modulate(1, ids, steps, (whole,), mods, modv, xm)
    for n, p in enumerate((1, 2, 0)):
        for cp in copies[n * len(plan) : (n + 1) * len(plan)]:
            cp.wait()
        lanes = slice(p * INNER, (p + 1) * INNER)
        acc = None if first else acc_in[:, lanes]
        for slot in range(n_slots):
            spot = offs[slots.index(slot)]
            cols = pl.ds(pl.multiple_of(spot - lax.rem(spot, CHUNK), 128), CHUNK)
            part = jnp.dot(
                xm[:, cols],
                w[p, slot * CHUNK : (slot + 1) * CHUNK, :],
                preferred_element_type=F32,
            )
            acc = part if acc is None else acc + part
        if not last:
            acc_out[:, lanes] = acc
        elif p == 0:
            normed_rotated(acc, cosr, sinr, q_out)
        elif p == 1:
            normed_rotated(acc, cosr, sinr, kv_out)
        else:
            kv_out[:, INNER:] = acc.astype(BF16)


def part_of_qkv(offs, plan, slots, pieces, ins, first=False, last=False):
    n, n_slots = len(pieces), max(slots) + 1
    hbm = pl.BlockSpec(memory_space=pltpu.HBM)
    vm = pl.BlockSpec(memory_space=pltpu.VMEM)
    sm = pl.BlockSpec(memory_space=pltpu.SMEM)
    acc = jax.ShapeDtypeStruct((ROWS, 3 * INNER), F32)
    scratch = [
        pltpu.VMEM((3, n_slots * CHUNK, INNER), BF16),
        pltpu.SemaphoreType.DMA((3 * len(plan),)),
    ]
    if first:
        in_specs = [sm, sm, vm, hbm]
        out_shape = (acc, jax.ShapeDtypeStruct((ROWS, WIDTH), BF16))
        scratch += [pltpu.VMEM((2, 2, 8, WIDTH), F32), pltpu.SemaphoreType.DMA((2,))]
    elif last:
        in_specs = [vm] * 4
        out_shape = (
            jax.ShapeDtypeStruct((ROWS, INNER), BF16),
            jax.ShapeDtypeStruct((ROWS, 2 * INNER), BF16),
        )
    else:
        in_specs, out_shape = [vm] * 2, acc
    return pl.pallas_call(
        functools.partial(part_kernel, plan, slots, n_slots, n, first, last),
        out_shape=out_shape,
        in_specs=[sm] + in_specs + [hbm] * n,
        scratch_shapes=scratch,
        compiler_params=pltpu.CompilerParams(vmem_limit_bytes=60 << 20),
        cost_estimate=pl.CostEstimate(
            flops=6 * ROWS * n_slots * CHUNK * INNER,
            bytes_accessed=6 * n_slots * CHUNK * INNER,
            transcendentals=0,
        ),
    )(offs, *ins, *pieces)


def kv_kernel(plan, n_pieces, n_x, ids, offs, steps, *refs):
    xs = refs[0:n_x]
    table, cosr, sinr = refs[n_x : n_x + 3]
    refs = refs[n_x + 3 :]
    pieces = refs[0:n_pieces]
    kv_out, xm = refs[n_pieces : n_pieces + 2]
    w_key, w_value, modv, mod_sems, sems = refs[n_pieces + 2 :]

    mods = start_modulation(steps, table, modv, mod_sems)
    key_copies = fetch(plan, offs, pieces, SLAB, w_key, sems, 0)
    value_copies = fetch(plan, offs, pieces, 2 * SLAB, w_value, sems, len(plan))
    modulate(n_x, ids, steps, xs, mods, modv, xm)
    for cp in key_copies:
        cp.wait()
    acc = jnp.dot(xm[...], w_key[...], preferred_element_type=F32)
    normed_rotated(acc, cosr, sinr, kv_out)
    for cp in value_copies:
        cp.wait()
    acc = jnp.dot(xm[...], w_value[...], preferred_element_type=F32)
    kv_out[:, INNER:] = acc.astype(BF16)


def project_kv(ids, offs, steps, plan, xs, table, cosr, sinr, pieces):
    n = len(pieces)
    hbm = pl.BlockSpec(memory_space=pltpu.HBM)
    vm = pl.BlockSpec(memory_space=pltpu.VMEM)
    sm = pl.BlockSpec(memory_space=pltpu.SMEM)
    return pl.pallas_call(
        functools.partial(kv_kernel, plan, n, len(xs)),
        out_shape=(
            jax.ShapeDtypeStruct((ROWS, 2 * INNER), BF16),
            jax.ShapeDtypeStruct((ROWS, WIDTH), BF16),
        ),
        in_specs=[sm] * 3 + [vm] * len(xs) + [hbm, vm, vm] + [hbm] * n,
        out_specs=(vm, vm),
        scratch_shapes=[
            pltpu.VMEM((WIDTH, INNER), BF16),
            pltpu.VMEM((WIDTH, INNER), BF16),
            pltpu.VMEM((2, 2, 8, WIDTH), F32),
            pltpu.SemaphoreType.DMA((2,)),
            pltpu.SemaphoreType.DMA((2 * len(plan),)),
        ],
        compiler_params=pltpu.CompilerParams(vmem_limit_bytes=60 << 20),
        cost_estimate=pl.CostEstimate(
            flops=4 * ROWS * WIDTH * INNER, bytes_accessed=WIDTH * INNER * 4, transcendentals=0
        ),
    )(ids, offs, steps, *xs, table, cosr, sinr, *pieces)


def project_q(offs, plan, xm, cosr, sinr, pieces):
    n = len(pieces)
    hbm = pl.BlockSpec(memory_space=pltpu.HBM)
    vm = pl.BlockSpec(memory_space=pltpu.VMEM)
    return pl.pallas_call(
        functools.partial(q_kernel, plan, n),
        out_shape=jax.ShapeDtypeStruct((ROWS, INNER), BF16),
        in_specs=[pl.BlockSpec(memory_space=pltpu.SMEM), vm, vm, vm] + [hbm] * n,
        out_specs=vm,
        scratch_shapes=[pltpu.VMEM((WIDTH, INNER), BF16), pltpu.SemaphoreType.DMA((len(plan),))],
        compiler_params=pltpu.CompilerParams(vmem_limit_bytes=60 << 20),
        cost_estimate=pl.CostEstimate(
            flops=2 * ROWS * WIDTH * INNER, bytes_accessed=WIDTH * INNER * 2, transcendentals=0
        ),
    )(offs, xm, cosr, sinr, *pieces)


def banded(ids, q, kv, kvc, kvb, att):
    row = lax.broadcasted_iota(jnp.int32, (ROWS, ROWS), 0)
    col = lax.broadcasted_iota(jnp.int32, (ROWS, ROWS), 1)
    core = ids[3]
    on_left = (row < BLK) | (col >= BLK)
    on_right = (row >= BLK) | (col < BLK)
    ok_c = (on_left & (core == 1)) | (on_right & (core == 0))
    inside = (ids[2] > 0) & (ids[2] < FRAMES - 1)
    ok_b = ((on_left & (core == 0)) | (on_right & (core == 1))) & inside
    nt = (((1,), (1,)), ((), ()))
    for h in range(3):
        lanes = slice(h * 128, (h + 1) * 128)
        vlanes = slice(INNER + h * 128, INNER + (h + 1) * 128)
        qh = q[:, lanes]
        es = []
        for ref, ok in ((kvc, ok_c), (kv, None), (kvb, ok_b)):
            s = lax.dot_general(qh, ref[:, lanes], nt, preferred_element_type=F32)
            e = jnp.exp(s * (1.0 / math.sqrt(HEAD_SIZE)))
            es.append(e if ok is None else jnp.where(ok, e, 0.0))
        total = jnp.sum(es[0] + es[1] + es[2], axis=1, keepdims=True)
        acc = jnp.zeros((ROWS, HEAD_SIZE), F32)
        for e, ref in zip(es, (kvc, kv, kvb)):
            acc = acc + jnp.dot(
                (e / total).astype(BF16), ref[:, vlanes], preferred_element_type=F32
            )
        att[:, lanes] = acc.astype(BF16)


def out_kernel(plan, n_pieces, ids, offs, *refs):
    n_in = 4
    pieces = refs[n_in : n_in + n_pieces]
    out, wo, att, sems = refs[n_in + n_pieces :]
    copies = fetch(plan, offs, pieces, 0, wo, sems, 0)
    banded(ids, *refs[:4], att)
    a = att[...]
    for cp in copies:
        cp.wait()
    nt = (((1,), (1,)), ((), ()))
    for j in range(HEADS_AXIS):
        prod = lax.dot_general(
            a, wo[j * CHUNK : (j + 1) * CHUNK, :], nt, preferred_element_type=F32
        )
        out[j] = prod.astype(BF16)


def project_out(ids, offs, plan, ins, pieces):
    n = len(pieces)
    vm = pl.BlockSpec(memory_space=pltpu.VMEM)
    sm = pl.BlockSpec(memory_space=pltpu.SMEM)
    return pl.pallas_call(
        functools.partial(out_kernel, plan, n),
        out_shape=jax.ShapeDtypeStruct((HEADS_AXIS, ROWS, CHUNK), BF16),
        in_specs=[sm, sm] + [vm] * len(ins) + [pl.BlockSpec(memory_space=pltpu.HBM)] * n,
        out_specs=vm,
        scratch_shapes=[
            pltpu.VMEM((WIDTH, INNER), BF16),
            pltpu.VMEM((ROWS, INNER), BF16),
            pltpu.SemaphoreType.DMA((len(plan),)),
        ],
        compiler_params=pltpu.CompilerParams(vmem_limit_bytes=60 << 20),
        cost_estimate=pl.CostEstimate(
            flops=2 * ROWS * WIDTH * INNER, bytes_accessed=WIDTH * INNER * 2, transcendentals=0
        ),
    )(ids, offs, *ins, *pieces)


def join_kernel(wq, wk, wv, wo, out):
    for i, ref in enumerate((wq, wk, wv, wo)):
        out[i * SLAB : (i + 1) * SLAB, :] = ref[...]


def joined(wq, wk, wv, wo):
    return pl.pallas_call(
        join_kernel,
        out_shape=jax.ShapeDtypeStruct((4 * SLAB, INNER), BF16),
        compiler_params=pltpu.CompilerParams(vmem_limit_bytes=60 << 20),
    )(wq, wk, wv, wo)


def update_kernel(first, ids, steps, sigma, table, got, base0, base1, *refs):
    if first:
        noise, out0, out1, gate, sems = refs
    else:
        out0, out1, gate, sems = refs
    copies = []
    for b in range(2):
        cols = pl.ds(pl.multiple_of(ids[4] * CHUNK, 128), CHUNK)
        eight = pl.ds(pl.multiple_of(steps[b] // 8 * 8, 8), 8)
        cp = pltpu.make_async_copy(table.at[2, eight, cols], gate.at[b], sems.at[b])
        cp.start()
        copies.append(cp)
    for b, base in enumerate((base0, base1)):
        rows = slice(b * BLK, (b + 1) * BLK)
        mixed = got[0, rows, :].astype(F32)
        for j in range(1, HEADS_AXIS):
            mixed = mixed + got[j, rows, :].astype(F32)
        copies[b].wait()
        wide = base[...].astype(F32)
        layer_out = wide + gate[b, pl.ds(lax.rem(steps[b], 8), 1), :] * mixed
        t = steps[b]
        following = wide + (sigma[t + 1] - sigma[t]) * layer_out
        if not first:
            out0[rows, :] = layer_out.astype(BF16)
            out1[rows, :] = following.astype(BF16)
        elif b == 0:
            out0[...] = jnp.where(ids[2] == 0, noise[...], following.astype(BF16))
        else:
            out1[...] = following.astype(BF16)


def update(ids, steps, sigma, table, got, base0, base1, *noise):
    first = len(noise) == 1
    vm = pl.BlockSpec(memory_space=pltpu.VMEM)
    sm = pl.BlockSpec(memory_space=pltpu.SMEM)
    hbm = pl.BlockSpec(memory_space=pltpu.HBM)
    shape = (BLK if first else ROWS, CHUNK)
    return pl.pallas_call(
        functools.partial(update_kernel, first),
        out_shape=(jax.ShapeDtypeStruct(shape, BF16),) * 2,
        in_specs=[sm, sm, sm, hbm] + [vm] * (3 + len(noise)),
        out_specs=(vm, vm),
        scratch_shapes=[pltpu.VMEM((2, 8, CHUNK), F32), pltpu.SemaphoreType.DMA((2,))],
        compiler_params=pltpu.CompilerParams(vmem_limit_bytes=16 << 20),
    )(ids, steps, sigma, table, got, base0, base1, *noise)


def per_device(
    queue,
    noise_block,
    w_query,
    w_key,
    w_value,
    w_output,
    mod_table,
    sigma_table,
    timestep_index,
    block_position,
):
    frame = lax.axis_index("frame")
    head = lax.axis_index("head")
    z, xh, core = frame // 4, (frame // 2) % 2, frame % 2
    y, xl = head // 2, head % 2
    ids = jnp.stack([y, xl, frame, core, head]).astype(jnp.int32)
    table = mod_table.transpose(1, 0, 2)
    half = HEAD_SIZE // 2
    freqs = 10000.0 ** (-jnp.arange(half, dtype=F32) / half)
    angles = block_position.astype(F32)[:, None] * freqs[None, :]
    cosr = jnp.concatenate([jnp.cos(angles), jnp.cos(angles)], axis=1)
    sinr = jnp.concatenate([-jnp.sin(angles), jnp.sin(angles)], axis=1)

    up = core == 0
    near = lambda d: jnp.where(up, z - d, z + d) % NZ
    far = lambda d: jnp.where(up, z + d, z - d) % NZ
    row_at = lambda zz, x, c: (zz * NXH + x) * 2 * SLAB + c * SLAB
    w = joined(w_query, w_key, w_value, w_output.T)
    cw = to_core(w)
    low, high = jnp.where(up, w, cw), jnp.where(up, cw, w)
    cut = lambda v: (v[: 3 * SLAB], v[3 * SLAB : 3 * SLAB + PART], v[3 * SLAB + PART :])
    (low, low_a, low_b), (high, high_a, high_b) = cut(low), cut(high)
    h1 = [jnp.concatenate([low, low_a, high, low_b], axis=0)]
    h1.append(along_z(h1[0]))
    xs = to_xh(after(w[: 3 * SLAB], cw))
    cxs = to_core(after(xs, h1[1]))
    low, high = jnp.where(up, xs, cxs), jnp.where(up, cxs, xs)
    h2 = [jnp.concatenate([low, high_a, high, high_b], axis=0)]
    h2.append(along_z(h2[0]))
    copies = jnp.broadcast_to(after(queue, cxs)[None], (HEADS_AXIS, ROWS, CHUNK))
    whole = lax.all_to_all(copies.reshape(-1, CHUNK), "head", 0, 0, tiled=True)

    qkv_at = [row_at(z, x, c) for x in (xh, 1 - xh) for c in (0, 1)]
    out_at = [row_at(z, xh, c) + e for c in (0, 1) for e in (0, PART)]
    both = ((near, core), (far, 1 - core))
    for d in range(1, 4):
        for x in (xh, 1 - xh):
            for side, c in both:
                first = c if d == 3 and x is not xh else 0
                qkv_at += [row_at(side(d), x, first), row_at(side(d), x, 1 - first)]
        for half in (0, 1):
            for side, c in both:
                first = c if d == 3 and half == 1 else 0
                out_at += [row_at(side(d), xh, half) + e * PART for e in (first, 1 - first)]
    for x in (xh, 1 - xh):
        qkv_at += [row_at(near(4), x, c) for c in (core, 1 - core)]
    for half in (0, 1):
        out_at += [row_at(near(4), xh, half) + e * PART for e in (core, 1 - core)]
    for side, c in both:
        out_at.append(row_at(z, 1 - xh, c))
        out_at += [row_at(side(d), 1 - xh, 0) for d in (1, 2)]
    for side, c in both:
        out_at.append(row_at(side(3), 1 - xh, 0))
        out_at += [row_at(side(3), 1 - xh, 1) + e * PART for e in (c, 1 - c)]
        out_at += [row_at(near(4), 1 - xh, half) + c * PART for half in (0, 1)]
    spots_1, spots_2, spots_3 = (
        jnp.stack(part).astype(jnp.int32) for part in (qkv_at[:12], qkv_at[12:20], qkv_at[20:])
    )
    qkv_spots = jnp.stack(qkv_at).astype(jnp.int32)
    out_spots = jnp.stack(out_at).astype(jnp.int32)

    mine = lambda v: jnp.where(up, v[:HALF], v[HALF:])
    other = lambda v: jnp.where(up, v[HALF:], v[:HALF])
    out_rows = lambda v: [v[3 * SLAB : HALF], v[HALF + 3 * SLAB :]]
    h1.append(along_z(h1[1]))
    h2.append(along_z(h2[1]))
    c1 = [to_core(h1[1])]
    c2 = [to_core(h2[1])]
    c1.append(to_core(after(h1[2], c1[0])))
    c2.append(to_core(after(h2[2], c2[0])))
    h1.append(along_z(after(h1[2], c1[0])))
    gated = after(h2[2], c2[0], ids, cosr, sinr, qkv_spots, spots_1, spots_2, spots_3, out_spots, whole)
    h2.append(along_z(mine(gated)))
    rest = along_z(other(gated))
    parts = [w[3 * SLAB :]]
    for d in (1, 2):
        parts += out_rows(h1[d]) + out_rows(h2[d])
    x_out = to_xh(jnp.concatenate(parts, axis=0))
    slab_plan = lambda held: tuple(
        (i, row, SLAB) for i, v in enumerate(held) for row in range(0, v.shape[0], HALF)
    )
    held = [h1[0], h2[0], h1[1], c1[0], h2[1], c2[0]]
    acc, xm = part_of_qkv(
        spots_1,
        slab_plan(held),
        (0,) * 4 + (1, 1, 2, 2) * 2,
        held,
        [ids, timestep_index, whole, table],
        first=True,
    )
    h2[3] = after(h2[3], acc)
    c1.append(to_core(after(h1[3], c1[1])))
    h1.append(along_z(after(mine(h1[3]), c1[1])))
    h2.append(along_z(after(h2[3], c2[1])))
    held = [h1[2], c1[1], h2[2], c2[1]]
    acc = part_of_qkv(spots_2, slab_plan(held), (0, 0, 1, 1) * 2, held, [xm, acc])
    h2[4] = after(h2[4], acc)
    c1.append(to_core(after(h1[4], c1[2])))
    c2.append(to_core(after(h2[3], c1[2])))
    c_rest = to_core(after(rest, c2[2]))
    c2.append(to_core(after(h2[4], c_rest)))
    parts = out_rows(h1[3])
    parts += [h[3 * SLAB :] for h in (h2[3], rest, h1[4], h2[4])]
    x_end = to_xh(jnp.concatenate(parts, axis=0))

    pieces = [h1[0], h2[0], h1[1], c1[0], h2[1], c2[0], h1[2], c1[1], h2[2], c2[1]]
    pieces += [h1[3], c1[2], h2[3], rest, c2[2], c_rest, h1[4], c1[3], h2[4], c2[3]]
    plan, out_plan = [], []
    for i, piece in enumerate(pieces):
        for row in range(0, piece.shape[0], HALF):
            plan.append((i, row, SLAB))
            out_plan.append((i, row + 3 * SLAB, PART))
    n = len(pieces)
    for i in (n, n + 1):
        out_plan += [(i, 0, SLAB), (i, SLAB, 2 * SLAB), (i, 3 * SLAB, 2 * SLAB)]
    for i in (n + 2, n + 3):
        out_plan += [(i, 0, SLAB)] + [(i, SLAB + e * PART, PART) for e in range(4)]
    plan, out_plan = tuple(plan), tuple(out_plan)

    def summed(q, kv, kvc, kvb, out_pieces):
        prod = project_out(ids, out_spots, out_plan, [q, kv, kvc, kvb], out_pieces)
        return lax.all_to_all(
            prod.reshape(HEADS_AXIS * ROWS, CHUNK), "head", 0, 0, tiled=True
        ).reshape(HEADS_AXIS, ROWS, CHUNK)

    held = pieces[10:]
    slots = (0, 0, 1, 1, 0, 0, 1, 1, 2, 2, 2, 2)
    q, kv = part_of_qkv(
        spots_3, slab_plan(held), slots, held, [xm, acc, cosr, sinr], last=True
    )
    kvb = to_bound(kv)
    kvc = to_core(kv)
    cx_out = to_core(after(x_out, kv))
    cx_end = to_core(after(x_end, kv))
    out_pieces = pieces + [x_out, cx_out, x_end, cx_end]
    got = summed(q, kv, kvc, kvb, out_pieces)
    leaving, a = update(
        ids, timestep_index, sigma_table, table, got, queue[:BLK], queue[BLK:], noise_block
    )

    def handed_back(v, cross):
        perm = []
        for f in range(FRAMES):
            for yy, ll in HEAD_COORDS:
                target = ((f - 1) % FRAMES) * HEADS_AXIS + head_of(yy, (ll + cross) % NXL)
                perm.append((f * HEADS_AXIS + head_of(yy, ll), target))
        return lax.ppermute(v, ("frame", "head"), perm)

    t = jnp.concatenate([a, to_xl(a)], axis=0)
    b = handed_back(leaving, 0)
    u = jnp.concatenate([b, handed_back(leaving, 1)], axis=0)
    xs = [t] + [along_y(t, k) for k in (1, 2, 3)] + [u] + [along_y(u, k) for k in (1, 2, 3)]
    kv, xm = project_kv(
        ids, qkv_spots, timestep_index, plan, xs, table, cosr, sinr, pieces
    )
    kvb = to_bound(kv)
    kvc = to_core(kv)
    q = project_q(qkv_spots, plan, xm, cosr, sinr, pieces)
    got = summed(q, kv, kvc, kvb, out_pieces)
    return update(ids, timestep_index, sigma_table, table, got, a, b)


def solution(mesh):
    in_specs = (
        P("frame", "head"),
        P(None, "head"),
        P("frame", "head"),
        P("frame", "head"),
        P("frame", "head"),
        P("head", "frame"),
        P(),
        P(),
        P("frame"),
        P("frame"),
    )
    out_specs = (P("frame", "head"), P("frame", "head"))
    return jax.shard_map(
        per_device, mesh=mesh, in_specs=in_specs, out_specs=out_specs, check_vma=False
    )
```

```python
import functools
import math

import jax
import jax.numpy as jnp
from jax import lax
from jax.experimental import pallas as pl
from jax.experimental.pallas import tpu as pltpu
from jax.sharding import PartitionSpec as P

HEAD_SIZE = 128
NZ, NXH, NCORE = 8, 2, 2
NY, NXL = 4, 2
FRAMES = NZ * NXH * NCORE
HEADS_AXIS = NY * NXL
INNER = 384
SLAB, PART = 160, 80
HALF = 3 * SLAB + PART
CHUNK = 640
WIDTH = 5120
ROWS = 128
BLK = 64
F32 = jnp.float32
BF16 = jnp.bfloat16


def frame_of(z, xh, core):
    return ((z % NZ) * NXH + xh) * NCORE + core


def head_of(y, xl):
    return (y % NY) * NXL + xl


FRAME_COORDS = [(z, xh, c) for z in range(NZ) for xh in range(NXH) for c in range(NCORE)]
HEAD_COORDS = [(y, xl) for y in range(NY) for xl in range(NXL)]


def to_core(v):
    return lax.ppermute(
        v, "frame", [(frame_of(z, x, c), frame_of(z, x, 1 - c)) for z, x, c in FRAME_COORDS]
    )


def to_xh(v):
    return lax.ppermute(
        v, "frame", [(frame_of(z, x, c), frame_of(z, 1 - x, c)) for z, x, c in FRAME_COORDS]
    )


def along_z(v):
    return lax.ppermute(
        v,
        "frame",
        [(frame_of(z, x, c), frame_of(z + 1 - 2 * c, x, c)) for z, x, c in FRAME_COORDS],
    )


def to_bound(v):
    pairs = [(i, i + 1) for i in range(1, FRAMES - 1, 2)]
    return lax.ppermute(v, "frame", pairs + [(j, i) for i, j in pairs])


def to_xl(v):
    return lax.ppermute(v, "head", [(head_of(y, l), head_of(y, 1 - l)) for y, l in HEAD_COORDS])


def along_y(v, k):
    return lax.ppermute(v, "head", [(head_of(y, l), head_of(y + k, l)) for y, l in HEAD_COORDS])


def after(value, *others):
    return lax.optimization_barrier((value,) + others)[0]


def normed_rotated(acc, cosr, sinr, out):
    for h in range(3):
        v = acc[:, h * 128 : (h + 1) * 128]
        v = v * lax.rsqrt(jnp.mean(v * v, axis=1, keepdims=True) + 1e-6)
        turned = pltpu.roll(v, 64, 1)
        for b in range(2):
            rows = slice(b * BLK, (b + 1) * BLK)
            res = v[rows] * cosr[b : b + 1, :] + turned[rows] * sinr[b : b + 1, :]
            out[rows, h * 128 : (h + 1) * 128] = res.astype(BF16)


def fetch(plan, offs, pieces, shift, dst, sems, slot):
    copies = []
    for i, (piece, low, rows) in enumerate(plan):
        cp = pltpu.make_async_copy(
            pieces[piece].at[pl.ds(low + shift, rows), :],
            dst.at[pl.ds(pl.multiple_of(offs[i], 16), rows), :],
            sems.at[slot + i],
        )
        cp.start()
        copies.append(cp)
    return copies


def q_kernel(plan, n_pieces, offs, xm, cosr, sinr, *refs):
    pieces = refs[:n_pieces]
    q_out, w, sems = refs[n_pieces:]
    for cp in fetch(plan, offs, pieces, 0, w, sems, 0):
        cp.wait()
    acc = jnp.dot(xm[...], w[...], preferred_element_type=F32)
    normed_rotated(acc, cosr, sinr, q_out)


def start_modulation(steps, table, modv, mod_sems):
    mods = []
    for b in range(2):
        eight = pl.ds(pl.multiple_of(steps[b] // 8 * 8, 8), 8)
        cp = pltpu.make_async_copy(table.at[0:2, eight, :], modv.at[b], mod_sems.at[b])
        cp.start()
        mods.append(cp)
    return mods


def modulate(n_x, ids, steps, xs, mods, modv, xm):
    y, xl = ids[0], ids[1]
    for b in range(2):
        spots = []
        for k in range(4):
            for r in range(2):
                j = lax.rem(y - k + NY, NY) * NXL + (xl + r - 2 * xl * r)
                if n_x == 1:
                    j = 2 * k + r
                    spots.append((j, xs[0], j * ROWS + b * BLK))
                elif b == 0:
                    spots.append((j, xs[k], r * BLK))
                else:
                    spots.append((j, xs[4 + k], r * BLK))

        def load(spot):
            return spot[1][spot[2] : spot[2] + BLK, :].astype(F32)

        def folded(v):
            t = v[:, 0:128]
            for i in range(1, 5):
                t = t + v[:, i * 128 : (i + 1) * 128]
            return t

        total = jnp.zeros((BLK, 128), F32)
        for s in spots:
            total = total + folded(load(s))
        mean = jnp.sum(total, axis=1, keepdims=True) * (1.0 / WIDTH)
        total = jnp.zeros((BLK, 128), F32)
        for s in spots:
            d = load(s) - mean
            total = total + folded(d * d)
        var = jnp.sum(total, axis=1, keepdims=True) * (1.0 / WIDTH)
        inv = lax.rsqrt(var + 1e-6)
        mods[b].wait()
        for s in spots:
            col = s[0] * CHUNK if n_x == 1 else pl.multiple_of(s[0] * CHUNK, 128)
            cols = pl.ds(col, CHUNK)
            row = pl.ds(lax.rem(steps[b], 8), 1)
            v = (load(s) - mean) * inv
            v = v * (1.0 + modv[b, 1, row, cols]) + modv[b, 0, row, cols]
            xm[b * BLK : (b + 1) * BLK, cols] = v.astype(BF16)


def kv_kernel(plan, n_pieces, n_x, ids, offs, steps, *refs):
    xs = refs[0:n_x]
    table, cosr, sinr = refs[n_x : n_x + 3]
    refs = refs[n_x + 3 :]
    pieces = refs[0:n_pieces]
    kv_out, xm = refs[n_pieces : n_pieces + 2]
    w_key, w_value, modv, mod_sems, sems = refs[n_pieces + 2 :]

    mods = start_modulation(steps, table, modv, mod_sems)
    key_copies = fetch(plan, offs, pieces, SLAB, w_key, sems, 0)
    value_copies = fetch(plan, offs, pieces, 2 * SLAB, w_value, sems, len(plan))
    modulate(n_x, ids, steps, xs, mods, modv, xm)
    for cp in key_copies:
        cp.wait()
    acc = jnp.dot(xm[...], w_key[...], preferred_element_type=F32)
    normed_rotated(acc, cosr, sinr, kv_out)
    for cp in value_copies:
        cp.wait()
    acc = jnp.dot(xm[...], w_value[...], preferred_element_type=F32)
    kv_out[:, INNER:] = acc.astype(BF16)


def project_kv(ids, offs, steps, plan, xs, table, cosr, sinr, pieces):
    n = len(pieces)
    hbm = pl.BlockSpec(memory_space=pltpu.HBM)
    vm = pl.BlockSpec(memory_space=pltpu.VMEM)
    sm = pl.BlockSpec(memory_space=pltpu.SMEM)
    return pl.pallas_call(
        functools.partial(kv_kernel, plan, n, len(xs)),
        out_shape=(
            jax.ShapeDtypeStruct((ROWS, 2 * INNER), BF16),
            jax.ShapeDtypeStruct((ROWS, WIDTH), BF16),
        ),
        in_specs=[sm] * 3 + [vm] * len(xs) + [hbm, vm, vm] + [hbm] * n,
        out_specs=(vm, vm),
        scratch_shapes=[
            pltpu.VMEM((WIDTH, INNER), BF16),
            pltpu.VMEM((WIDTH, INNER), BF16),
            pltpu.VMEM((2, 2, 8, WIDTH), F32),
            pltpu.SemaphoreType.DMA((2,)),
            pltpu.SemaphoreType.DMA((2 * len(plan),)),
        ],
        compiler_params=pltpu.CompilerParams(vmem_limit_bytes=60 << 20),
        cost_estimate=pl.CostEstimate(
            flops=4 * ROWS * WIDTH * INNER, bytes_accessed=WIDTH * INNER * 4, transcendentals=0
        ),
    )(ids, offs, steps, *xs, table, cosr, sinr, *pieces)


def project_q(offs, plan, xm, cosr, sinr, pieces):
    n = len(pieces)
    hbm = pl.BlockSpec(memory_space=pltpu.HBM)
    vm = pl.BlockSpec(memory_space=pltpu.VMEM)
    return pl.pallas_call(
        functools.partial(q_kernel, plan, n),
        out_shape=jax.ShapeDtypeStruct((ROWS, INNER), BF16),
        in_specs=[pl.BlockSpec(memory_space=pltpu.SMEM), vm, vm, vm] + [hbm] * n,
        out_specs=vm,
        scratch_shapes=[pltpu.VMEM((WIDTH, INNER), BF16), pltpu.SemaphoreType.DMA((len(plan),))],
        compiler_params=pltpu.CompilerParams(vmem_limit_bytes=60 << 20),
        cost_estimate=pl.CostEstimate(
            flops=2 * ROWS * WIDTH * INNER, bytes_accessed=WIDTH * INNER * 2, transcendentals=0
        ),
    )(offs, xm, cosr, sinr, *pieces)


def banded(ids, q, kv, kvc, kvb, att):
    row = lax.broadcasted_iota(jnp.int32, (ROWS, ROWS), 0)
    col = lax.broadcasted_iota(jnp.int32, (ROWS, ROWS), 1)
    core = ids[3]
    on_left = (row < BLK) | (col >= BLK)
    on_right = (row >= BLK) | (col < BLK)
    ok_c = (on_left & (core == 1)) | (on_right & (core == 0))
    inside = (ids[2] > 0) & (ids[2] < FRAMES - 1)
    ok_b = ((on_left & (core == 0)) | (on_right & (core == 1))) & inside
    nt = (((1,), (1,)), ((), ()))
    for h in range(3):
        lanes = slice(h * 128, (h + 1) * 128)
        vlanes = slice(INNER + h * 128, INNER + (h + 1) * 128)
        qh = q[:, lanes]
        es = []
        for ref, ok in ((kvc, ok_c), (kv, None), (kvb, ok_b)):
            s = lax.dot_general(qh, ref[:, lanes], nt, preferred_element_type=F32)
            e = jnp.exp(s * (1.0 / math.sqrt(HEAD_SIZE)))
            es.append(e if ok is None else jnp.where(ok, e, 0.0))
        total = jnp.sum(es[0] + es[1] + es[2], axis=1, keepdims=True)
        acc = jnp.zeros((ROWS, HEAD_SIZE), F32)
        for e, ref in zip(es, (kvc, kv, kvb)):
            acc = acc + jnp.dot(
                (e / total).astype(BF16), ref[:, vlanes], preferred_element_type=F32
            )
        att[:, lanes] = acc.astype(BF16)


def out_kernel(plan, n_pieces, ids, offs, *refs):
    n_in = 4
    pieces = refs[n_in : n_in + n_pieces]
    out, wo, att, sems = refs[n_in + n_pieces :]
    copies = fetch(plan, offs, pieces, 0, wo, sems, 0)
    banded(ids, *refs[:4], att)
    a = att[...]
    for cp in copies:
        cp.wait()
    nt = (((1,), (1,)), ((), ()))
    for j in range(HEADS_AXIS):
        prod = lax.dot_general(
            a, wo[j * CHUNK : (j + 1) * CHUNK, :], nt, preferred_element_type=F32
        )
        out[j] = prod.astype(BF16)


def project_out(ids, offs, plan, ins, pieces):
    n = len(pieces)
    vm = pl.BlockSpec(memory_space=pltpu.VMEM)
    sm = pl.BlockSpec(memory_space=pltpu.SMEM)
    return pl.pallas_call(
        functools.partial(out_kernel, plan, n),
        out_shape=jax.ShapeDtypeStruct((HEADS_AXIS, ROWS, CHUNK), BF16),
        in_specs=[sm, sm] + [vm] * len(ins) + [pl.BlockSpec(memory_space=pltpu.HBM)] * n,
        out_specs=vm,
        scratch_shapes=[
            pltpu.VMEM((WIDTH, INNER), BF16),
            pltpu.VMEM((ROWS, INNER), BF16),
            pltpu.SemaphoreType.DMA((len(plan),)),
        ],
        compiler_params=pltpu.CompilerParams(vmem_limit_bytes=60 << 20),
        cost_estimate=pl.CostEstimate(
            flops=2 * ROWS * WIDTH * INNER, bytes_accessed=WIDTH * INNER * 2, transcendentals=0
        ),
    )(ids, offs, *ins, *pieces)


def join_kernel(wq, wk, wv, wo, out):
    for i, ref in enumerate((wq, wk, wv, wo)):
        out[i * SLAB : (i + 1) * SLAB, :] = ref[...]


def joined(wq, wk, wv, wo):
    return pl.pallas_call(
        join_kernel,
        out_shape=jax.ShapeDtypeStruct((4 * SLAB, INNER), BF16),
        compiler_params=pltpu.CompilerParams(vmem_limit_bytes=60 << 20),
    )(wq, wk, wv, wo)


def update_kernel(first, ids, steps, sigma, table, got, base0, base1, *refs):
    if first:
        noise, out0, out1, gate, sems = refs
    else:
        out0, out1, gate, sems = refs
    copies = []
    for b in range(2):
        cols = pl.ds(pl.multiple_of(ids[4] * CHUNK, 128), CHUNK)
        eight = pl.ds(pl.multiple_of(steps[b] // 8 * 8, 8), 8)
        cp = pltpu.make_async_copy(table.at[2, eight, cols], gate.at[b], sems.at[b])
        cp.start()
        copies.append(cp)
    for b, base in enumerate((base0, base1)):
        rows = slice(b * BLK, (b + 1) * BLK)
        mixed = got[0, rows, :].astype(F32)
        for j in range(1, HEADS_AXIS):
            mixed = mixed + got[j, rows, :].astype(F32)
        copies[b].wait()
        wide = base[...].astype(F32)
        layer_out = wide + gate[b, pl.ds(lax.rem(steps[b], 8), 1), :] * mixed
        t = steps[b]
        following = wide + (sigma[t + 1] - sigma[t]) * layer_out
        if not first:
            out0[rows, :] = layer_out.astype(BF16)
            out1[rows, :] = following.astype(BF16)
        elif b == 0:
            out0[...] = jnp.where(ids[2] == 0, noise[...], following.astype(BF16))
        else:
            out1[...] = following.astype(BF16)


def update(ids, steps, sigma, table, got, base0, base1, *noise):
    first = len(noise) == 1
    vm = pl.BlockSpec(memory_space=pltpu.VMEM)
    sm = pl.BlockSpec(memory_space=pltpu.SMEM)
    hbm = pl.BlockSpec(memory_space=pltpu.HBM)
    shape = (BLK if first else ROWS, CHUNK)
    return pl.pallas_call(
        functools.partial(update_kernel, first),
        out_shape=(jax.ShapeDtypeStruct(shape, BF16),) * 2,
        in_specs=[sm, sm, sm, hbm] + [vm] * (3 + len(noise)),
        out_specs=(vm, vm),
        scratch_shapes=[pltpu.VMEM((2, 8, CHUNK), F32), pltpu.SemaphoreType.DMA((2,))],
        compiler_params=pltpu.CompilerParams(vmem_limit_bytes=16 << 20),
    )(ids, steps, sigma, table, got, base0, base1, *noise)


def per_device(
    queue,
    noise_block,
    w_query,
    w_key,
    w_value,
    w_output,
    mod_table,
    sigma_table,
    timestep_index,
    block_position,
):
    frame = lax.axis_index("frame")
    head = lax.axis_index("head")
    z, xh, core = frame // 4, (frame // 2) % 2, frame % 2
    y, xl = head // 2, head % 2
    ids = jnp.stack([y, xl, frame, core, head]).astype(jnp.int32)
    table = mod_table.transpose(1, 0, 2)
    half = HEAD_SIZE // 2
    freqs = 10000.0 ** (-jnp.arange(half, dtype=F32) / half)
    angles = block_position.astype(F32)[:, None] * freqs[None, :]
    cosr = jnp.concatenate([jnp.cos(angles), jnp.cos(angles)], axis=1)
    sinr = jnp.concatenate([-jnp.sin(angles), jnp.sin(angles)], axis=1)

    up = core == 0
    near = lambda d: jnp.where(up, z - d, z + d) % NZ
    far = lambda d: jnp.where(up, z + d, z - d) % NZ
    row_at = lambda zz, x, c: (zz * NXH + x) * 2 * SLAB + c * SLAB
    w = joined(w_query, w_key, w_value, w_output.T)
    cw = to_core(w)
    low, high = jnp.where(up, w, cw), jnp.where(up, cw, w)
    cut = lambda v: (v[: 3 * SLAB], v[3 * SLAB : 3 * SLAB + PART], v[3 * SLAB + PART :])
    (low, low_a, low_b), (high, high_a, high_b) = cut(low), cut(high)
    h1 = [jnp.concatenate([low, low_a, high, low_b], axis=0)]
    h1.append(along_z(h1[0]))
    xs = to_xh(after(w[: 3 * SLAB], cw))
    cxs = to_core(after(xs, h1[1]))
    low, high = jnp.where(up, xs, cxs), jnp.where(up, cxs, xs)
    h2 = [jnp.concatenate([low, high_a, high, high_b], axis=0)]
    h2.append(along_z(h2[0]))
    copies = jnp.broadcast_to(after(queue, cxs)[None], (HEADS_AXIS, ROWS, CHUNK))
    whole = lax.all_to_all(copies.reshape(-1, CHUNK), "head", 0, 0, tiled=True)

    qkv_at = [row_at(z, x, c) for x in (xh, 1 - xh) for c in (0, 1)]
    out_at = [row_at(z, xh, c) + e for c in (0, 1) for e in (0, PART)]
    both = ((near, core), (far, 1 - core))
    for d in range(1, 4):
        for x in (xh, 1 - xh):
            for side, c in both:
                first = c if d == 3 and x is not xh else 0
                qkv_at += [row_at(side(d), x, first), row_at(side(d), x, 1 - first)]
        for half in (0, 1):
            for side, c in both:
                first = c if d == 3 and half == 1 else 0
                out_at += [row_at(side(d), xh, half) + e * PART for e in (first, 1 - first)]
    for x in (xh, 1 - xh):
        qkv_at += [row_at(near(4), x, c) for c in (core, 1 - core)]
    for half in (0, 1):
        out_at += [row_at(near(4), xh, half) + e * PART for e in (core, 1 - core)]
    for side, c in both:
        out_at.append(row_at(z, 1 - xh, c))
        out_at += [row_at(side(d), 1 - xh, 0) for d in (1, 2)]
    for side, c in both:
        out_at.append(row_at(side(3), 1 - xh, 0))
        out_at += [row_at(side(3), 1 - xh, 1) + e * PART for e in (c, 1 - c)]
        out_at += [row_at(near(4), 1 - xh, half) + c * PART for half in (0, 1)]
    qkv_spots = jnp.stack(qkv_at).astype(jnp.int32)
    out_spots = jnp.stack(out_at).astype(jnp.int32)

    mine = lambda v: jnp.where(up, v[:HALF], v[HALF:])
    other = lambda v: jnp.where(up, v[HALF:], v[:HALF])
    out_rows = lambda v: [v[3 * SLAB : HALF], v[HALF + 3 * SLAB :]]
    h1.append(along_z(h1[1]))
    h2.append(along_z(h2[1]))
    c1 = [to_core(h1[1])]
    c2 = [to_core(h2[1])]
    c1.append(to_core(after(h1[2], c1[0])))
    c2.append(to_core(after(h2[2], c2[0])))
    h1.append(along_z(after(h1[2], c1[0])))
    gated = after(h2[2], c2[0], ids, cosr, sinr, qkv_spots, out_spots, whole)
    h2.append(along_z(mine(gated)))
    rest = along_z(other(gated))
    parts = [w[3 * SLAB :]]
    for d in (1, 2):
        parts += out_rows(h1[d]) + out_rows(h2[d])
    x_out = to_xh(jnp.concatenate(parts, axis=0))
    c1.append(to_core(after(h1[3], c1[1])))
    h1.append(along_z(after(mine(h1[3]), c1[1])))
    h2.append(along_z(after(h2[3], c2[1])))
    c1.append(to_core(after(h1[4], c1[2])))
    c2.append(to_core(after(h2[3], c1[2])))
    c_rest = to_core(after(rest, c2[2]))
    c2.append(to_core(after(h2[4], c_rest)))
    parts = out_rows(h1[3])
    parts += [h[3 * SLAB :] for h in (h2[3], rest, h1[4], h2[4])]
    x_end = to_xh(jnp.concatenate(parts, axis=0))

    pieces = [h1[0], h2[0], h1[1], c1[0], h2[1], c2[0], h1[2], c1[1], h2[2], c2[1]]
    pieces += [h1[3], c1[2], h2[3], rest, c2[2], c_rest, h1[4], c1[3], h2[4], c2[3]]
    plan, out_plan = [], []
    for i, piece in enumerate(pieces):
        for row in range(0, piece.shape[0], HALF):
            plan.append((i, row, SLAB))
            out_plan.append((i, row + 3 * SLAB, PART))
    n = len(pieces)
    for i in (n, n + 1):
        out_plan += [(i, 0, SLAB), (i, SLAB, 2 * SLAB), (i, 3 * SLAB, 2 * SLAB)]
    for i in (n + 2, n + 3):
        out_plan += [(i, 0, SLAB)] + [(i, SLAB + e * PART, PART) for e in range(4)]
    plan, out_plan = tuple(plan), tuple(out_plan)

    def summed(q, kv, kvc, kvb, out_pieces):
        prod = project_out(ids, out_spots, out_plan, [q, kv, kvc, kvb], out_pieces)
        return lax.all_to_all(
            prod.reshape(HEADS_AXIS * ROWS, CHUNK), "head", 0, 0, tiled=True
        ).reshape(HEADS_AXIS, ROWS, CHUNK)

    kv, xm = project_kv(
        ids, qkv_spots, timestep_index, plan, [whole], table, cosr, sinr, pieces
    )
    kvb = to_bound(kv)
    kvc = to_core(kv)
    q = project_q(qkv_spots, plan, xm, cosr, sinr, pieces)
    cx_out = to_core(after(x_out, kv))
    cx_end = to_core(after(x_end, kv))
    out_pieces = pieces + [x_out, cx_out, x_end, cx_end]
    got = summed(q, kv, kvc, kvb, out_pieces)
    leaving, a = update(
        ids, timestep_index, sigma_table, table, got, queue[:BLK], queue[BLK:], noise_block
    )

    def handed_back(v, cross):
        perm = []
        for f in range(FRAMES):
            for yy, ll in HEAD_COORDS:
                target = ((f - 1) % FRAMES) * HEADS_AXIS + head_of(yy, (ll + cross) % NXL)
                perm.append((f * HEADS_AXIS + head_of(yy, ll), target))
        return lax.ppermute(v, ("frame", "head"), perm)

    t = jnp.concatenate([a, to_xl(a)], axis=0)
    b = handed_back(leaving, 0)
    u = jnp.concatenate([b, handed_back(leaving, 1)], axis=0)
    xs = [t] + [along_y(t, k) for k in (1, 2, 3)] + [u] + [along_y(u, k) for k in (1, 2, 3)]
    kv, xm = project_kv(
        ids, qkv_spots, timestep_index, plan, xs, table, cosr, sinr, pieces
    )
    kvb = to_bound(kv)
    kvc = to_core(kv)
    q = project_q(qkv_spots, plan, xm, cosr, sinr, pieces)
    got = summed(q, kv, kvc, kvb, out_pieces)
    return update(ids, timestep_index, sigma_table, table, got, a, b)


def solution(mesh):
    in_specs = (
        P("frame", "head"),
        P(None, "head"),
        P("frame", "head"),
        P("frame", "head"),
        P("frame", "head"),
        P("head", "frame"),
        P(),
        P(),
        P("frame"),
        P("frame"),
    )
    out_specs = (P("frame", "head"), P("frame", "head"))
    return jax.shard_map(
        per_device, mesh=mesh, in_specs=in_specs, out_specs=out_specs, check_vma=False
    )
```

```python
import functools
import math

import jax
import jax.numpy as jnp
from jax import lax
from jax.experimental import pallas as pl
from jax.experimental.pallas import tpu as pltpu
from jax.sharding import PartitionSpec as P

HEAD_SIZE = 128
NZ, NXH, NCORE = 8, 2, 2
NY, NXL = 4, 2
FRAMES = NZ * NXH * NCORE
HEADS_AXIS = NY * NXL
INNER = 384
SLAB, PART = 160, 80
HALF = 3 * SLAB + PART
CHUNK = 640
WIDTH = 5120
ROWS = 128
BLK = 64
F32 = jnp.float32
BF16 = jnp.bfloat16


def frame_of(z, xh, core):
    return ((z % NZ) * NXH + xh) * NCORE + core


def head_of(y, xl):
    return (y % NY) * NXL + xl


FRAME_COORDS = [(z, xh, c) for z in range(NZ) for xh in range(NXH) for c in range(NCORE)]
HEAD_COORDS = [(y, xl) for y in range(NY) for xl in range(NXL)]


def to_core(v):
    return lax.ppermute(
        v, "frame", [(frame_of(z, x, c), frame_of(z, x, 1 - c)) for z, x, c in FRAME_COORDS]
    )


def to_xh(v):
    return lax.ppermute(
        v, "frame", [(frame_of(z, x, c), frame_of(z, 1 - x, c)) for z, x, c in FRAME_COORDS]
    )


def along_z(v):
    return lax.ppermute(
        v,
        "frame",
        [(frame_of(z, x, c), frame_of(z + 1 - 2 * c, x, c)) for z, x, c in FRAME_COORDS],
    )


def to_bound(v):
    pairs = [(i, i + 1) for i in range(1, FRAMES - 1, 2)]
    return lax.ppermute(v, "frame", pairs + [(j, i) for i, j in pairs])


def to_xl(v):
    return lax.ppermute(v, "head", [(head_of(y, l), head_of(y, 1 - l)) for y, l in HEAD_COORDS])


def along_y(v, k):
    return lax.ppermute(v, "head", [(head_of(y, l), head_of(y + k, l)) for y, l in HEAD_COORDS])


def after(value, *others):
    return lax.optimization_barrier((value,) + others)[0]


def normed_rotated(acc, cosr, sinr, out):
    for h in range(3):
        v = acc[:, h * 128 : (h + 1) * 128]
        v = v * lax.rsqrt(jnp.mean(v * v, axis=1, keepdims=True) + 1e-6)
        turned = pltpu.roll(v, 64, 1)
        for b in range(2):
            rows = slice(b * BLK, (b + 1) * BLK)
            res = v[rows] * cosr[b : b + 1, :] + turned[rows] * sinr[b : b + 1, :]
            out[rows, h * 128 : (h + 1) * 128] = res.astype(BF16)


def fetch(plan, offs, pieces, shift, dst, sems, slot):
    copies = []
    for i, (piece, low, rows) in enumerate(plan):
        cp = pltpu.make_async_copy(
            pieces[piece].at[pl.ds(low + shift, rows), :],
            dst.at[pl.ds(pl.multiple_of(offs[i], 16), rows), :],
            sems.at[slot + i],
        )
        cp.start()
        copies.append(cp)
    return copies


def q_kernel(plan, n_pieces, offs, xm, cosr, sinr, *refs):
    pieces = refs[:n_pieces]
    q_out, w, sems = refs[n_pieces:]
    for cp in fetch(plan, offs, pieces, 0, w, sems, 0):
        cp.wait()
    acc = jnp.dot(xm[...], w[...], preferred_element_type=F32)
    normed_rotated(acc, cosr, sinr, q_out)


def start_modulation(steps, table, modv, mod_sems):
    mods = []
    for b in range(2):
        eight = pl.ds(pl.multiple_of(steps[b] // 8 * 8, 8), 8)
        cp = pltpu.make_async_copy(table.at[0:2, eight, :], modv.at[b], mod_sems.at[b])
        cp.start()
        mods.append(cp)
    return mods


def modulate(n_x, ids, steps, xs, mods, modv, xm):
    y, xl = ids[0], ids[1]
    for b in range(2):
        spots = []
        for k in range(4):
            for r in range(2):
                j = lax.rem(y - k + NY, NY) * NXL + (xl + r - 2 * xl * r)
                if n_x == 1:
                    j = 2 * k + r
                    spots.append((j, xs[0], j * ROWS + b * BLK))
                elif b == 0:
                    spots.append((j, xs[k], r * BLK))
                else:
                    spots.append((j, xs[4 + k], r * BLK))

        def load(spot):
            return spot[1][spot[2] : spot[2] + BLK, :].astype(F32)

        def folded(v):
            t = v[:, 0:128]
            for i in range(1, 5):
                t = t + v[:, i * 128 : (i + 1) * 128]
            return t

        total = jnp.zeros((BLK, 128), F32)
        for s in spots:
            total = total + folded(load(s))
        mean = jnp.sum(total, axis=1, keepdims=True) * (1.0 / WIDTH)
        total = jnp.zeros((BLK, 128), F32)
        for s in spots:
            d = load(s) - mean
            total = total + folded(d * d)
        var = jnp.sum(total, axis=1, keepdims=True) * (1.0 / WIDTH)
        inv = lax.rsqrt(var + 1e-6)
        mods[b].wait()
        for s in spots:
            col = s[0] * CHUNK if n_x == 1 else pl.multiple_of(s[0] * CHUNK, 128)
            cols = pl.ds(col, CHUNK)
            row = pl.ds(lax.rem(steps[b], 8), 1)
            v = (load(s) - mean) * inv
            v = v * (1.0 + modv[b, 1, row, cols]) + modv[b, 0, row, cols]
            xm[b * BLK : (b + 1) * BLK, cols] = v.astype(BF16)


def kv_kernel(plan, n_pieces, n_x, ids, offs, steps, *refs):
    xs = refs[0:n_x]
    table, cosr, sinr = refs[n_x : n_x + 3]
    refs = refs[n_x + 3 :]
    pieces = refs[0:n_pieces]
    kv_out, xm = refs[n_pieces : n_pieces + 2]
    w_key, w_value, modv, mod_sems, sems = refs[n_pieces + 2 :]

    mods = start_modulation(steps, table, modv, mod_sems)
    key_copies = fetch(plan, offs, pieces, SLAB, w_key, sems, 0)
    value_copies = fetch(plan, offs, pieces, 2 * SLAB, w_value, sems, len(plan))
    modulate(n_x, ids, steps, xs, mods, modv, xm)
    for cp in key_copies:
        cp.wait()
    acc = jnp.dot(xm[...], w_key[...], preferred_element_type=F32)
    normed_rotated(acc, cosr, sinr, kv_out)
    for cp in value_copies:
        cp.wait()
    acc = jnp.dot(xm[...], w_value[...], preferred_element_type=F32)
    kv_out[:, INNER:] = acc.astype(BF16)


def project_kv(ids, offs, steps, plan, xs, table, cosr, sinr, pieces):
    n = len(pieces)
    hbm = pl.BlockSpec(memory_space=pltpu.HBM)
    vm = pl.BlockSpec(memory_space=pltpu.VMEM)
    sm = pl.BlockSpec(memory_space=pltpu.SMEM)
    return pl.pallas_call(
        functools.partial(kv_kernel, plan, n, len(xs)),
        out_shape=(
            jax.ShapeDtypeStruct((ROWS, 2 * INNER), BF16),
            jax.ShapeDtypeStruct((ROWS, WIDTH), BF16),
        ),
        in_specs=[sm] * 3 + [vm] * len(xs) + [hbm, vm, vm] + [hbm] * n,
        out_specs=(vm, vm),
        scratch_shapes=[
            pltpu.VMEM((WIDTH, INNER), BF16),
            pltpu.VMEM((WIDTH, INNER), BF16),
            pltpu.VMEM((2, 2, 8, WIDTH), F32),
            pltpu.SemaphoreType.DMA((2,)),
            pltpu.SemaphoreType.DMA((2 * len(plan),)),
        ],
        compiler_params=pltpu.CompilerParams(vmem_limit_bytes=60 << 20),
        cost_estimate=pl.CostEstimate(
            flops=4 * ROWS * WIDTH * INNER, bytes_accessed=WIDTH * INNER * 4, transcendentals=0
        ),
    )(ids, offs, steps, *xs, table, cosr, sinr, *pieces)


def project_q(offs, plan, xm, cosr, sinr, pieces):
    n = len(pieces)
    hbm = pl.BlockSpec(memory_space=pltpu.HBM)
    vm = pl.BlockSpec(memory_space=pltpu.VMEM)
    return pl.pallas_call(
        functools.partial(q_kernel, plan, n),
        out_shape=jax.ShapeDtypeStruct((ROWS, INNER), BF16),
        in_specs=[pl.BlockSpec(memory_space=pltpu.SMEM), vm, vm, vm] + [hbm] * n,
        out_specs=vm,
        scratch_shapes=[pltpu.VMEM((WIDTH, INNER), BF16), pltpu.SemaphoreType.DMA((len(plan),))],
        compiler_params=pltpu.CompilerParams(vmem_limit_bytes=60 << 20),
        cost_estimate=pl.CostEstimate(
            flops=2 * ROWS * WIDTH * INNER, bytes_accessed=WIDTH * INNER * 2, transcendentals=0
        ),
    )(offs, xm, cosr, sinr, *pieces)


def banded(ids, q, kv, kvc, kvb, att):
    row = lax.broadcasted_iota(jnp.int32, (ROWS, ROWS), 0)
    col = lax.broadcasted_iota(jnp.int32, (ROWS, ROWS), 1)
    core = ids[3]
    on_left = (row < BLK) | (col >= BLK)
    on_right = (row >= BLK) | (col < BLK)
    ok_c = (on_left & (core == 1)) | (on_right & (core == 0))
    inside = (ids[2] > 0) & (ids[2] < FRAMES - 1)
    ok_b = ((on_left & (core == 0)) | (on_right & (core == 1))) & inside
    nt = (((1,), (1,)), ((), ()))
    for h in range(3):
        lanes = slice(h * 128, (h + 1) * 128)
        vlanes = slice(INNER + h * 128, INNER + (h + 1) * 128)
        qh = q[:, lanes]
        es = []
        for ref, ok in ((kvc, ok_c), (kv, None), (kvb, ok_b)):
            s = lax.dot_general(qh, ref[:, lanes], nt, preferred_element_type=F32)
            e = jnp.exp(s * (1.0 / math.sqrt(HEAD_SIZE)))
            es.append(e if ok is None else jnp.where(ok, e, 0.0))
        total = jnp.sum(es[0] + es[1] + es[2], axis=1, keepdims=True)
        acc = jnp.zeros((ROWS, HEAD_SIZE), F32)
        for e, ref in zip(es, (kvc, kv, kvb)):
            acc = acc + jnp.dot(
                (e / total).astype(BF16), ref[:, vlanes], preferred_element_type=F32
            )
        att[:, lanes] = acc.astype(BF16)


def out_kernel(plan, n_pieces, ids, offs, *refs):
    n_in = 4
    pieces = refs[n_in : n_in + n_pieces]
    out, wo, att, sems = refs[n_in + n_pieces :]
    copies = fetch(plan, offs, pieces, 0, wo, sems, 0)
    banded(ids, *refs[:4], att)
    a = att[...]
    for cp in copies:
        cp.wait()
    nt = (((1,), (1,)), ((), ()))
    for j in range(HEADS_AXIS):
        prod = lax.dot_general(
            a, wo[j * CHUNK : (j + 1) * CHUNK, :], nt, preferred_element_type=F32
        )
        out[j] = prod.astype(BF16)


def project_out(ids, offs, plan, ins, pieces):
    n = len(pieces)
    vm = pl.BlockSpec(memory_space=pltpu.VMEM)
    sm = pl.BlockSpec(memory_space=pltpu.SMEM)
    return pl.pallas_call(
        functools.partial(out_kernel, plan, n),
        out_shape=jax.ShapeDtypeStruct((HEADS_AXIS, ROWS, CHUNK), BF16),
        in_specs=[sm, sm] + [vm] * len(ins) + [pl.BlockSpec(memory_space=pltpu.HBM)] * n,
        out_specs=vm,
        scratch_shapes=[
            pltpu.VMEM((WIDTH, INNER), BF16),
            pltpu.VMEM((ROWS, INNER), BF16),
            pltpu.SemaphoreType.DMA((len(plan),)),
        ],
        compiler_params=pltpu.CompilerParams(vmem_limit_bytes=60 << 20),
        cost_estimate=pl.CostEstimate(
            flops=2 * ROWS * WIDTH * INNER, bytes_accessed=WIDTH * INNER * 2, transcendentals=0
        ),
    )(ids, offs, *ins, *pieces)


def join_kernel(wq, wk, wv, wo, out):
    for i, ref in enumerate((wq, wk, wv, wo)):
        out[i * SLAB : (i + 1) * SLAB, :] = ref[...]


def joined(wq, wk, wv, wo):
    return pl.pallas_call(
        join_kernel,
        out_shape=jax.ShapeDtypeStruct((4 * SLAB, INNER), BF16),
        compiler_params=pltpu.CompilerParams(vmem_limit_bytes=60 << 20),
    )(wq, wk, wv, wo)


def gate_kernel(ids, steps, table, out, gate, sems):
    copies = []
    for b in range(2):
        cols = pl.ds(pl.multiple_of(ids[4] * CHUNK, 128), CHUNK)
        eight = pl.ds(pl.multiple_of(steps[b] // 8 * 8, 8), 8)
        cp = pltpu.make_async_copy(table.at[2, eight, cols], gate.at[b], sems.at[b])
        cp.start()
        copies.append(cp)
    for b in range(2):
        copies[b].wait()
        out[b : b + 1, :] = gate[b, pl.ds(lax.rem(steps[b], 8), 1), :]


def gate_rows(ids, steps, table):
    sm = pl.BlockSpec(memory_space=pltpu.SMEM)
    return pl.pallas_call(
        gate_kernel,
        out_shape=jax.ShapeDtypeStruct((2, CHUNK), F32),
        in_specs=[sm, sm, pl.BlockSpec(memory_space=pltpu.HBM)],
        scratch_shapes=[pltpu.VMEM((2, 8, CHUNK), F32), pltpu.SemaphoreType.DMA((2,))],
        compiler_params=pltpu.CompilerParams(vmem_limit_bytes=60 << 20),
    )(ids, steps, table)


def update_kernel(first, ids, steps, sigma, gate, got, base0, base1, *refs):
    if first:
        noise, out0, out1 = refs
    else:
        out0, out1 = refs
    for b, base in enumerate((base0, base1)):
        rows = slice(b * BLK, (b + 1) * BLK)
        mixed = got[0, rows, :].astype(F32)
        for j in range(1, HEADS_AXIS):
            mixed = mixed + got[j, rows, :].astype(F32)
        wide = base[...].astype(F32)
        layer_out = wide + gate[b : b + 1, :] * mixed
        t = steps[b]
        following = wide + (sigma[t + 1] - sigma[t]) * layer_out
        if not first:
            out0[rows, :] = layer_out.astype(BF16)
            out1[rows, :] = following.astype(BF16)
        elif b == 0:
            out0[...] = jnp.where(ids[2] == 0, noise[...], following.astype(BF16))
        else:
            out1[...] = following.astype(BF16)


def update(ids, steps, sigma, gate, got, base0, base1, *noise):
    first = len(noise) == 1
    vm = pl.BlockSpec(memory_space=pltpu.VMEM)
    sm = pl.BlockSpec(memory_space=pltpu.SMEM)
    shape = (BLK if first else ROWS, CHUNK)
    return pl.pallas_call(
        functools.partial(update_kernel, first),
        out_shape=(jax.ShapeDtypeStruct(shape, BF16),) * 2,
        in_specs=[sm, sm, sm] + [vm] * (4 + len(noise)),
        out_specs=(vm, vm),
        compiler_params=pltpu.CompilerParams(vmem_limit_bytes=16 << 20),
    )(ids, steps, sigma, gate, got, base0, base1, *noise)


def per_device(
    queue,
    noise_block,
    w_query,
    w_key,
    w_value,
    w_output,
    mod_table,
    sigma_table,
    timestep_index,
    block_position,
):
    frame = lax.axis_index("frame")
    head = lax.axis_index("head")
    z, xh, core = frame // 4, (frame // 2) % 2, frame % 2
    y, xl = head // 2, head % 2
    ids = jnp.stack([y, xl, frame, core, head]).astype(jnp.int32)
    table = mod_table.transpose(1, 0, 2)
    gate = gate_rows(ids, timestep_index, table)
    half = HEAD_SIZE // 2
    freqs = 10000.0 ** (-jnp.arange(half, dtype=F32) / half)
    angles = block_position.astype(F32)[:, None] * freqs[None, :]
    cosr = jnp.concatenate([jnp.cos(angles), jnp.cos(angles)], axis=1)
    sinr = jnp.concatenate([-jnp.sin(angles), jnp.sin(angles)], axis=1)

    up = core == 0
    near = lambda d: jnp.where(up, z - d, z + d) % NZ
    far = lambda d: jnp.where(up, z + d, z - d) % NZ
    row_at = lambda zz, x, c: (zz * NXH + x) * 2 * SLAB + c * SLAB
    w = joined(w_query, w_key, w_value, w_output.T)
    cw = to_core(w)
    low, high = jnp.where(up, w, cw), jnp.where(up, cw, w)
    cut = lambda v: (v[: 3 * SLAB], v[3 * SLAB : 3 * SLAB + PART], v[3 * SLAB + PART :])
    (low, low_a, low_b), (high, high_a, high_b) = cut(low), cut(high)
    h1 = [jnp.concatenate([low, low_a, high, low_b], axis=0)]
    h1.append(along_z(h1[0]))
    xs = to_xh(after(w[: 3 * SLAB], cw))
    cxs = to_core(after(xs, h1[1]))
    low, high = jnp.where(up, xs, cxs), jnp.where(up, cxs, xs)
    h2 = [jnp.concatenate([low, high_a, high, high_b], axis=0)]
    h2.append(along_z(h2[0]))
    copies = jnp.broadcast_to(after(queue, cxs)[None], (HEADS_AXIS, ROWS, CHUNK))
    whole = lax.all_to_all(copies.reshape(-1, CHUNK), "head", 0, 0, tiled=True)

    qkv_at = [row_at(z, x, c) for x in (xh, 1 - xh) for c in (0, 1)]
    out_at = [row_at(z, xh, c) + e for c in (0, 1) for e in (0, PART)]
    both = ((near, core), (far, 1 - core))
    for d in range(1, 4):
        for x in (xh, 1 - xh):
            for side, c in both:
                first = c if d == 3 and x is not xh else 0
                qkv_at += [row_at(side(d), x, first), row_at(side(d), x, 1 - first)]
        for half in (0, 1):
            for side, c in both:
                first = c if d == 3 and half == 1 else 0
                out_at += [row_at(side(d), xh, half) + e * PART for e in (first, 1 - first)]
    for x in (xh, 1 - xh):
        qkv_at += [row_at(near(4), x, c) for c in (core, 1 - core)]
    for half in (0, 1):
        out_at += [row_at(near(4), xh, half) + e * PART for e in (core, 1 - core)]
    for side, c in both:
        out_at.append(row_at(z, 1 - xh, c))
        out_at += [row_at(side(d), 1 - xh, 0) for d in (1, 2)]
    for side, c in both:
        out_at.append(row_at(side(3), 1 - xh, 0))
        out_at += [row_at(side(3), 1 - xh, 1) + e * PART for e in (c, 1 - c)]
        out_at += [row_at(near(4), 1 - xh, half) + c * PART for half in (0, 1)]
    qkv_spots = jnp.stack(qkv_at).astype(jnp.int32)
    out_spots = jnp.stack(out_at).astype(jnp.int32)

    mine = lambda v: jnp.where(up, v[:HALF], v[HALF:])
    other = lambda v: jnp.where(up, v[HALF:], v[:HALF])
    out_rows = lambda v: [v[3 * SLAB : HALF], v[HALF + 3 * SLAB :]]
    h1.append(along_z(h1[1]))
    h2.append(along_z(h2[1]))
    c1 = [to_core(h1[1])]
    c2 = [to_core(h2[1])]
    c1.append(to_core(after(h1[2], c1[0])))
    c2.append(to_core(after(h2[2], c2[0])))
    h1.append(along_z(after(h1[2], c1[0])))
    gated = after(h2[2], c2[0], ids, cosr, sinr, qkv_spots, out_spots, whole, gate)
    h2.append(along_z(mine(gated)))
    rest = along_z(other(gated))
    parts = [w[3 * SLAB :]]
    for d in (1, 2):
        parts += out_rows(h1[d]) + out_rows(h2[d])
    x_out = to_xh(jnp.concatenate(parts, axis=0))
    c1.append(to_core(after(h1[3], c1[1])))
    h1.append(along_z(after(mine(h1[3]), c1[1])))
    h2.append(along_z(after(h2[3], c2[1])))
    c1.append(to_core(after(h1[4], c1[2])))
    c2.append(to_core(after(h2[3], c1[2])))
    c_rest = to_core(after(rest, c2[2]))
    c2.append(to_core(after(h2[4], c_rest)))
    parts = out_rows(h1[3])
    parts += [h[3 * SLAB :] for h in (h2[3], rest, h1[4], h2[4])]
    x_end = to_xh(jnp.concatenate(parts, axis=0))

    pieces = [h1[0], h2[0], h1[1], c1[0], h2[1], c2[0], h1[2], c1[1], h2[2], c2[1]]
    pieces += [h1[3], c1[2], h2[3], rest, c2[2], c_rest, h1[4], c1[3], h2[4], c2[3]]
    plan, out_plan = [], []
    for i, piece in enumerate(pieces):
        for row in range(0, piece.shape[0], HALF):
            plan.append((i, row, SLAB))
            out_plan.append((i, row + 3 * SLAB, PART))
    n = len(pieces)
    for i in (n, n + 1):
        out_plan += [(i, 0, SLAB), (i, SLAB, 2 * SLAB), (i, 3 * SLAB, 2 * SLAB)]
    for i in (n + 2, n + 3):
        out_plan += [(i, 0, SLAB)] + [(i, SLAB + e * PART, PART) for e in range(4)]
    plan, out_plan = tuple(plan), tuple(out_plan)

    def summed(q, kv, kvc, kvb, out_pieces):
        prod = project_out(ids, out_spots, out_plan, [q, kv, kvc, kvb], out_pieces)
        return lax.all_to_all(
            prod.reshape(HEADS_AXIS * ROWS, CHUNK), "head", 0, 0, tiled=True
        ).reshape(HEADS_AXIS, ROWS, CHUNK)

    kv, xm = project_kv(
        ids, qkv_spots, timestep_index, plan, [whole], table, cosr, sinr, pieces
    )
    kvb = to_bound(kv)
    kvc = to_core(kv)
    q = project_q(qkv_spots, plan, xm, cosr, sinr, pieces)
    cx_out = to_core(after(x_out, kv))
    cx_end = to_core(after(x_end, kv))
    out_pieces = pieces + [x_out, cx_out, x_end, cx_end]
    got = summed(q, kv, kvc, kvb, out_pieces)
    leaving, a = update(
        ids, timestep_index, sigma_table, gate, got, queue[:BLK], queue[BLK:], noise_block
    )

    def handed_back(v, cross):
        perm = []
        for f in range(FRAMES):
            for yy, ll in HEAD_COORDS:
                target = ((f - 1) % FRAMES) * HEADS_AXIS + head_of(yy, (ll + cross) % NXL)
                perm.append((f * HEADS_AXIS + head_of(yy, ll), target))
        return lax.ppermute(v, ("frame", "head"), perm)

    t = jnp.concatenate([a, to_xl(a)], axis=0)
    b = handed_back(leaving, 0)
    u = jnp.concatenate([b, handed_back(leaving, 1)], axis=0)
    xs = [t] + [along_y(t, k) for k in (1, 2, 3)] + [u] + [along_y(u, k) for k in (1, 2, 3)]
    kv, xm = project_kv(
        ids, qkv_spots, timestep_index, plan, xs, table, cosr, sinr, pieces
    )
    kvb = to_bound(kv)
    kvc = to_core(kv)
    q = project_q(qkv_spots, plan, xm, cosr, sinr, pieces)
    got = summed(q, kv, kvc, kvb, out_pieces)
    return update(ids, timestep_index, sigma_table, gate, got, a, b)


def solution(mesh):
    in_specs = (
        P("frame", "head"),
        P(None, "head"),
        P("frame", "head"),
        P("frame", "head"),
        P("frame", "head"),
        P("head", "frame"),
        P(),
        P(),
        P("frame"),
        P("frame"),
    )
    out_specs = (P("frame", "head"), P("frame", "head"))
    return jax.shard_map(
        per_device, mesh=mesh, in_specs=in_specs, out_specs=out_specs, check_vma=False
    )
```
